256 devices in a mesh: chan: 32 (over y_hi, z, core), day: 8 (over y_lo, x).
Axes of the slice: x: 4, y: 4 (y_hi: 2, y_lo: 2; y = y_hi * 2 + y_lo), z: 8, core: 2. Of those that a mesh axis runs over, the one named last changes fastest.
Arguments:
- spectra: bfloat16 [8, 512, 80, 256], P('day', 'chan'), may hold values from -500 to 500
Outputs:
- stacked: float32 [512, 512, 256], P('day', 'chan')
The draws below stay inside these ranges and needn't reach their ends.
All inputs are finite; a program needn't handle non-finite values.
Results may differ from the reference program's by a relative error of at most 0.0023.
Values may be sent and summed in bfloat16 or wider, within the bound.
A program may use at most 128 MiB of HBM per device.

```python
import math
import jax
import jax.numpy as jnp
from jax import lax

F = 128
LAGS = 256
W = 80
CH_DEV = 16
C = 512
DAYS = 8
N_CHAN = 32


def draw_spectra(key, part):
    key = jax.random.fold_in(key, 11)
    base_key, row_key, col_key = jax.random.split(key, 3)
    shape = (DAYS, C, W, 2 * F)
    row_scale = jnp.exp(jax.random.uniform(row_key, (DAYS, C, W, 1), jnp.float32, 0.0, math.log(10.0)))
    col_scale = jnp.exp(jax.random.uniform(col_key, (1, C, 1, 2 * F), jnp.float32, 0.0, math.log(10.0)))
    values = jax.random.normal(base_key, shape, jnp.float32)
    return (jnp.clip(values, -5.0, 5.0) * row_scale * col_scale).astype(jnp.bfloat16)


def setup_inputs(seed: int = 0) -> dict:
    splits = jax.random.split(jax.random.key(seed), 2)
    spectra = draw_spectra(jax.random.fold_in(splits[1], 71), 0)
    return dict(spectra=spectra)


def freq_taper(bins):
    freq_index = jnp.arange(bins, dtype=jnp.float32)
    half_taper = 0.54 - 0.46 * jnp.cos(2.0 * jnp.pi * (freq_index + 0.5) / bins)
    return jnp.concatenate([half_taper, half_taper])

def whiten(spectra):
    values = spectra.astype(jnp.float32)
    bins = values.shape[-1] // 2
    band_power = lax.optimization_barrier(jnp.sum(values * values, axis=-1, keepdims=True)) / bins + 1e-06
    return (values * freq_taper(bins) / jnp.sqrt(band_power)).astype(jnp.bfloat16)

def lag_matrix(bins):
    lag_count = 2 * bins
    freq_index = jnp.arange(bins, dtype=jnp.int32)
    lag_index = jnp.arange(lag_count, dtype=jnp.int32) - bins
    wound = jnp.mod(freq_index[:, None] * lag_index[None, :], lag_count)
    phase_angle = 2.0 * jnp.pi / lag_count * wound.astype(jnp.float32)
    return jnp.concatenate([jnp.cos(phase_angle), -jnp.sin(phase_angle)], axis=0)

def cross_spectra(far_rows, near_rows):
    far_vals = far_rows.astype(jnp.float32)
    near_vals = near_rows.astype(jnp.float32)
    bins = far_vals.shape[-1] // 2
    windows = far_vals.shape[-2]
    far_re, far_im = (far_vals[..., :bins], far_vals[..., bins:])
    near_re, near_im = (near_vals[..., :bins], near_vals[..., bins:])
    real_part = jnp.einsum('djwf,diwf->jif', far_re, near_re) + jnp.einsum('djwf,diwf->jif', far_im, near_im)
    imag_part = jnp.einsum('djwf,diwf->jif', far_re, near_im) - jnp.einsum('djwf,diwf->jif', far_im, near_re)
    return jnp.concatenate([real_part, imag_part], axis=-1) / windows

def to_lags(cross, table):
    flat = cross.reshape(-1, cross.shape[-1])
    lagged = jnp.dot(flat, table, precision=lax.Precision.HIGHEST, preferred_element_type=jnp.float32)
    return lagged.reshape(cross.shape[:-1] + (table.shape[1],))

def reference(spectra):
    white = whiten(spectra)
    table = lag_matrix(F)
    blocks = jnp.moveaxis(white.reshape(DAYS, N_CHAN, CH_DEV, W, 2 * F), 1, 0)

    def one_block(far_rows):
        return to_lags(cross_spectra(far_rows, white), table) / DAYS
    stacked = lax.map(one_block, blocks)
    return stacked.reshape(C, C, LAGS)
```

```python
import jax
import jax.numpy as jnp
import numpy as np
from jax import lax
from jax.experimental import pallas as pl
from jax.experimental.pallas import tpu as pltpu
from jax.sharding import PartitionSpec as P

F32 = jnp.float32
BF16 = jnp.bfloat16
MESH = pl.DeviceIdType.MESH
BINS = 128
LAGS = 256
WINDOWS = 80
CH = 16
DAYS = 8
CHIPS = 16
HEAD = 64
KB = 10
NT = (((1,), (1,)), ((), ()))


def taper_table():
    f = np.arange(BINS, dtype=np.float64)
    taper = 0.54 - 0.46 * np.cos(2.0 * np.pi * (f + 0.5) / BINS)
    return np.ascontiguousarray(np.broadcast_to(taper[:, None], (BINS, 128)).astype(np.float32))


def lag_tables():
    slot = np.arange(BINS)
    chip = slot % CHIPS
    f = (slot // CHIPS) * CHIPS + (chip % 4) * 4 + chip // 4
    wound = (f[:, None] * (np.arange(LAGS)[None, :] - BINS)) % LAGS
    angle = 2.0 * np.pi / LAGS * wound
    table = np.concatenate([np.cos(angle), -np.sin(angle)], axis=0) / (WINDOWS * DAYS)
    table = table.astype(np.float32)
    high = table.astype(jnp.bfloat16)
    low = (table - high.astype(np.float32)).astype(jnp.bfloat16)
    return high, low


def kernel(
    x_ref, taper_ref, high_ref, low_ref, out_ref,
    head_f, tail_f, send_a, recv_a, mix_f, send_b, recv_b, near, far,
    send_c, recv_c, recv_d, lag_f, lag_rows,
    a_send, a_recv, b_send, b_recv, s_send, s_recv, c_send, c_recv, d_send, d_recv,
):
    c = lax.axis_index("chan")
    d = lax.axis_index("day")
    core = lax.rem(c, 2)
    chip = c // 2
    chip_lo = lax.rem(chip, 4)
    chip_hi = chip // 4

    barrier = pltpu.get_barrier_semaphore()
    for e in range(1, DAYS):
        pl.semaphore_signal(barrier, inc=1, device_id={"day": d ^ e}, device_id_type=MESH)
    for m in range(1, CHIPS):
        pl.semaphore_signal(barrier, inc=1, device_id={"chan": c ^ (2 * m)}, device_id_type=MESH)
    pl.semaphore_signal(barrier, inc=1, device_id={"chan": c ^ 1}, device_id_type=MESH)

    lane = lax.broadcasted_iota(jnp.int32, (1, 128), 1)
    group = lane // 32
    first16 = lax.rem(lane, 32) < 16
    sign64 = jnp.where(lane < 64, -1.0, 1.0).astype(F32)
    sign16 = jnp.where(first16, -1.0, 1.0).astype(F32)

    def swap16(v):
        return jnp.where(first16, pltpu.roll(v, 112, 1), pltpu.roll(v, 16, 1))

    def whiten(g, carry):
        taper = taper_ref[...]
        tails = []
        for u in range(4):
            ch = g * 4 + u
            v = x_ref[0, ch].astype(F32)
            t = jnp.concatenate([v[:HEAD, :128], v[:HEAD, 128:]], axis=0).T
            part = jnp.sum(t * t, axis=0, keepdims=True)
            power = (part + pltpu.roll(part, 64, 1)) / BINS + 1e-06
            head_f[pl.ds(ch, 128, stride=CH), :] = t * taper * (1.0 / jnp.sqrt(power))
            tails += [v[HEAD:, :128], v[HEAD:, 128:]]
        t = jnp.concatenate(tails, axis=0).T
        part = jnp.sum(t * t, axis=0, keepdims=True)
        power = (part + swap16(part)) / BINS + 1e-06
        tail_f[pl.ds(g, 128, stride=4), :] = t * taper * (1.0 / jnp.sqrt(power))
        return carry

    lax.fori_loop(0, 4, whiten, 0)

    def pack(b, carry):
        send_a[b, 0:64, :] = head_f[pl.ds(pl.multiple_of(b * 64, 64), 64), :].astype(BF16)
        send_a[b, 64:80, :] = tail_f[pl.ds(pl.multiple_of(b * 16, 16), 16), :].astype(BF16)
        return carry

    lax.fori_loop(0, 32, pack, 0)

    pl.semaphore_wait(barrier, 23)

    for s in range(4):
        q = chip_lo ^ s
        for e in range(1, DAYS):
            to = d ^ e
            pltpu.make_async_remote_copy(
                send_a.at[to * 4 + q], recv_a.at[q, d], a_send, a_recv.at[s],
                device_id={"day": to}, device_id_type=MESH,
            ).start()
    for s in range(4):
        q = chip_lo ^ s
        recv_a[q, d] = send_a[d * 4 + q]

    def forward(src):
        return pltpu.make_async_remote_copy(
            recv_b.at[core, src], recv_b.at[core, src], s_send, s_recv.at[src],
            device_id={"chan": c ^ 1}, device_id_type=MESH,
        )

    def spread(side, src, mine):
        row = pl.multiple_of((src // 2) * 128 + lax.rem(src, 2) * 32 + side * 16, 16)
        for k in range(KB):
            z = recv_b[side, src, k]
            zf = z.astype(F32)
            turned = pltpu.roll(zf, 64, 1) * sign64 if k < DAYS else swap16(zf) * sign16
            far[pl.ds(row, 16), k * 128 : (k + 1) * 128] = z
            far[pl.ds(row + 64, 16), k * 128 : (k + 1) * 128] = turned.astype(BF16)
            if mine:
                near[pl.ds(pl.multiple_of(src * 16, 16), 16), k * 128 : (k + 1) * 128] = z

    for s in range(4):
        q = chip_lo ^ s
        pltpu.make_async_copy(
            recv_a.at[q, pl.ds(0, 7)], recv_a.at[q, pl.ds(0, 7)], a_recv.at[s]
        ).wait()
        for h in range(2):
            tiles = [recv_a[q, 4 * h + n, 64:80, :].astype(F32) for n in range(4)]
            for u in range(4):
                mixed = tiles[u]
                for n in range(4):
                    if n != u:
                        moved = pltpu.roll(tiles[n], (32 * (n - u)) % 128, 1)
                        mixed = jnp.where(group == n, moved, mixed)
                mix_f[pl.ds(h * 64 + u, 16, stride=4), :] = mixed
        for jj in range(4):
            j = chip_hi ^ jj
            to = 4 * j + q
            rows = pl.ds(pl.multiple_of(j * 16, 16), 16)
            tail_rows = [pl.ds(pl.multiple_of(h * 64 + j * 16, 16), 16) for h in range(2)]
            if s == 0 and jj == 0:
                recv_b[core, chip, 0:8] = recv_a[q, :, rows, :]
                for h in range(2):
                    recv_b[core, chip, 8 + h] = mix_f[tail_rows[h], :].astype(BF16)
                forward(chip).start()
            else:
                send_b[to, 0:8] = recv_a[q, :, rows, :]
                for h in range(2):
                    send_b[to, 8 + h] = mix_f[tail_rows[h], :].astype(BF16)
                pltpu.make_async_remote_copy(
                    send_b.at[to], recv_b.at[core, chip], b_send, b_recv.at[chip],
                    device_id={"chan": to * 2 + core}, device_id_type=MESH,
                ).start()

    spread(core, chip, True)

    def arrive(n, carry):
        src = chip ^ (lax.rem(n, 4) * 4 + n // 4)
        pltpu.make_async_copy(recv_b.at[core, src], recv_b.at[core, src], b_recv.at[src]).wait()
        forward(src).start()
        spread(core, src, True)
        return carry

    lax.fori_loop(1, CHIPS, arrive, 0)

    def arrive_other(n, carry):
        src = chip ^ (lax.rem(n, 4) * 4 + n // 4)
        side = 1 - core
        pltpu.make_async_copy(recv_b.at[side, src], recv_b.at[side, src], s_recv.at[src]).wait()
        spread(side, src, False)
        return carry

    lax.fori_loop(0, CHIPS, arrive_other, 0)

    for s in range(4):
        p = (d // 2) ^ s
        prod = lax.dot_general(
            near[...], far[pl.ds(pl.multiple_of(p * 256, 256), 256), :], NT,
            preferred_element_type=F32,
        )
        for e in range(2):
            send_c[2 * p + e] = prod[:, e * 128 : (e + 1) * 128].astype(BF16).reshape(CHIPS, 16, 128)
        recv_c[pl.ds(2 * p, 2), chip] = send_c[pl.ds(2 * p, 2), chip]
        for m in range(1, CHIPS):
            to = chip ^ m
            pltpu.make_async_remote_copy(
                send_c.at[pl.ds(2 * p, 2), to], recv_c.at[pl.ds(2 * p, 2), chip],
                c_send.at[s], c_recv.at[s],
                device_id={"chan": to * 2 + core}, device_id_type=MESH,
            ).start()

    for s in range(4):
        some = recv_c.at[pl.ds(0, 2), pl.ds(0, 15)]
        pltpu.make_async_copy(some, some, c_recv.at[s]).wait()
        for e in range(2):
            to = d ^ (2 * s + e)
            if s == 0 and e == 0:
                lag_f[pl.ds(pl.multiple_of(d * 256, 256), 256), :] = (
                    recv_c[d].reshape(256, 128).astype(F32)
                )
            else:
                pltpu.make_async_remote_copy(
                    recv_c.at[to], recv_d.at[d], d_send, d_recv.at[d],
                    device_id={"day": to}, device_id_type=MESH,
                ).start()
    for e in range(1, DAYS):
        src = d ^ e
        pltpu.make_async_copy(recv_d.at[src], recv_d.at[src], d_recv.at[src]).wait()
        lag_f[pl.ds(pl.multiple_of(src * 256, 256), 256), :] = (
            recv_d[src].reshape(256, 128).astype(F32)
        )

    for n in range(4):
        for u in range(4):
            t = lag_f[pl.ds(n * 4 + u, 128, stride=16), :].T.astype(BF16)
            lag_rows[u * 64 : (u + 1) * 64, 0:128] = t[0:64]
            lag_rows[u * 64 : (u + 1) * 64, 128:256] = t[64:128]
        rows = lag_rows[...]
        lags = jnp.dot(rows, high_ref[...], preferred_element_type=F32)
        lags = lags + jnp.dot(rows, low_ref[...], preferred_element_type=F32)
        for u in range(4):
            for h in range(2):
                out_ref[pl.ds((n * 4 + u) * 2 + h, 64, stride=32), :] = (
                    lags[u * 64 : (u + 1) * 64, h * 128 : (h + 1) * 128]
                )

    sent = send_a.at[pl.ds(0, 28)]
    pltpu.make_async_copy(sent, sent, a_send).wait()
    sent = send_b.at[pl.ds(0, 15)]
    pltpu.make_async_copy(sent, sent, b_send).wait()
    sent = recv_b.at[0]
    pltpu.make_async_copy(sent, sent, s_send).wait()
    for s in range(4):
        sent = send_c.at[pl.ds(0, 2), pl.ds(0, 15)]
        pltpu.make_async_copy(sent, sent, c_send.at[s]).wait()
    sent = recv_d.at[pl.ds(0, 7)]
    pltpu.make_async_copy(sent, sent, d_send).wait()


def shards(spectra):
    high, low = lag_tables()
    dma = pltpu.SemaphoreType.DMA
    out = pl.pallas_call(
        kernel,
        out_shape=jax.ShapeDtypeStruct((2048, 128), F32),
        in_specs=[pl.BlockSpec(memory_space=pltpu.VMEM)] * 4,
        out_specs=pl.BlockSpec(memory_space=pltpu.VMEM),
        scratch_shapes=[
            pltpu.VMEM((2048, 128), F32),
            pltpu.VMEM((512, 128), F32),
            pltpu.VMEM((32, 80, 128), BF16),
            pltpu.VMEM((4, 8, 80, 128), BF16),
            pltpu.VMEM((128, 128), F32),
            pltpu.VMEM((CHIPS, KB, 16, 128), BF16),
            pltpu.VMEM((2, CHIPS, KB, 16, 128), BF16),
            pltpu.VMEM((256, KB * 128), BF16),
            pltpu.VMEM((1024, KB * 128), BF16),
            pltpu.VMEM((DAYS, CHIPS, 16, 128), BF16),
            pltpu.VMEM((DAYS, CHIPS, 16, 128), BF16),
            pltpu.VMEM((DAYS, CHIPS, 16, 128), BF16),
            pltpu.VMEM((2048, 128), F32),
            pltpu.VMEM((256, 256), BF16),
            dma,
            dma((4,)),
            dma,
            dma((CHIPS,)),
            dma,
            dma((CHIPS,)),
            dma((4,)),
            dma((4,)),
            dma,
            dma((DAYS,)),
        ],
        compiler_params=pltpu.CompilerParams(
            collective_id=0, has_side_effects=True, vmem_limit_bytes=40 << 20
        ),
    )(spectra, jnp.asarray(taper_table()), jnp.asarray(high), jnp.asarray(low))
    return out.reshape(64, 16, 256)


def solution(mesh):
    return jax.shard_map(
        shards,
        mesh=mesh,
        in_specs=(P("day", "chan", None, None),),
        out_specs=P("day", "chan", None),
        check_vma=False,
    )
```

```python
import jax
import jax.numpy as jnp
import numpy as np
from jax import lax
from jax.experimental import pallas as pl
from jax.experimental.pallas import tpu as pltpu
from jax.sharding import PartitionSpec as P

F32 = jnp.float32
BF16 = jnp.bfloat16
MESH = pl.DeviceIdType.MESH
BINS = 128
LAGS = 256
WINDOWS = 80
CH = 16
DAYS = 8
CHIPS = 16
HEAD = 64
KB = 10
NT = (((1,), (1,)), ((), ()))


def taper_table():
    f = np.arange(BINS, dtype=np.float64)
    taper = 0.54 - 0.46 * np.cos(2.0 * np.pi * (f + 0.5) / BINS)
    return np.ascontiguousarray(np.broadcast_to(taper[:, None], (BINS, 128)).astype(np.float32))


def lag_tables():
    slot = np.arange(BINS)
    chip = slot % CHIPS
    f = (slot // CHIPS) * CHIPS + (chip % 4) * 4 + chip // 4
    wound = (f[:, None] * (np.arange(LAGS)[None, :] - BINS)) % LAGS
    angle = 2.0 * np.pi / LAGS * wound
    table = np.concatenate([np.cos(angle), -np.sin(angle)], axis=0) / (WINDOWS * DAYS)
    table = table.astype(np.float32)
    high = table.astype(jnp.bfloat16)
    low = (table - high.astype(np.float32)).astype(jnp.bfloat16)
    return high, low


def kernel(
    x_hbm, taper_hbm, tables_hbm, out_ref,
    x_ref, taper_ref, tables, head_f, tail_f, send_a, recv_a, mix_f, send_b, recv_b, near, far,
    send_c, recv_d, lag_f, lag_rows, out_f,
    x_in, taper_in, tables_in,    a_send, a_recv, b_send, b_recv, s_send, s_recv, d_send, d_recv,
):
    c = lax.axis_index("chan")
    d = lax.axis_index("day")
    core = lax.rem(c, 2)
    chip = c // 2
    chip_lo = lax.rem(chip, 4)
    chip_hi = chip // 4

    x_copies = [
        pltpu.make_async_copy(
            x_hbm.at[0, pl.ds(4 * g, 4)], x_ref.at[pl.ds(4 * g, 4)], x_in.at[g]
        )
        for g in range(4)
    ]
    taper_copy = pltpu.make_async_copy(taper_hbm, taper_ref, taper_in)
    tables_copy = pltpu.make_async_copy(tables_hbm, tables, tables_in)
    x_copies[0].start()
    taper_copy.start()
    for g in range(1, 4):
        x_copies[g].start()
    tables_copy.start()

    barrier = pltpu.get_barrier_semaphore()
    for e in range(1, DAYS):
        pl.semaphore_signal(barrier, inc=1, device_id={"day": d ^ e}, device_id_type=MESH)
    for m in range(1, CHIPS):
        pl.semaphore_signal(barrier, inc=1, device_id={"chan": c ^ (2 * m)}, device_id_type=MESH)
    pl.semaphore_signal(barrier, inc=1, device_id={"chan": c ^ 1}, device_id_type=MESH)

    lane = lax.broadcasted_iota(jnp.int32, (1, 128), 1)
    group = lane // 32
    first16 = lax.rem(lane, 32) < 16
    sign64 = jnp.where(lane < 64, -1.0, 1.0).astype(F32)
    sign16 = jnp.where(first16, -1.0, 1.0).astype(F32)

    def swap16(v):
        return jnp.where(first16, pltpu.roll(v, 112, 1), pltpu.roll(v, 16, 1))

    def whiten(g):
        taper = taper_ref[...]
        tails = []
        for u in range(4):
            ch = g * 4 + u
            v = x_ref[ch].astype(F32)
            t = jnp.concatenate([v[:HEAD, :128], v[:HEAD, 128:]], axis=0).T
            part = jnp.sum(t * t, axis=0, keepdims=True)
            power = (part + pltpu.roll(part, 64, 1)) / BINS + 1e-06
            head_f[pl.ds(ch, 128, stride=CH), :] = t * taper * (1.0 / jnp.sqrt(power))
            tails += [v[HEAD:, :128], v[HEAD:, 128:]]
        t = jnp.concatenate(tails, axis=0).T
        part = jnp.sum(t * t, axis=0, keepdims=True)
        power = (part + swap16(part)) / BINS + 1e-06
        tail_f[pl.ds(g, 128, stride=4), :] = t * taper * (1.0 / jnp.sqrt(power))

    taper_copy.wait()
    for g in range(4):
        x_copies[g].wait()
        whiten(g)

    def pack(b, carry):
        send_a[b, 0:64, :] = head_f[pl.ds(pl.multiple_of(b * 64, 64), 64), :].astype(BF16)
        send_a[b, 64:80, :] = tail_f[pl.ds(pl.multiple_of(b * 16, 16), 16), :].astype(BF16)
        return carry

    lax.fori_loop(0, 32, pack, 0)

    pl.semaphore_wait(barrier, 23)

    for s in range(4):
        q = chip_lo ^ s
        for e in range(1, DAYS):
            to = d ^ e
            pltpu.make_async_remote_copy(
                send_a.at[to * 4 + q], recv_a.at[q, d], a_send, a_recv.at[s],
                device_id={"day": to}, device_id_type=MESH,
            ).start()
    for s in range(4):
        q = chip_lo ^ s
        recv_a[q, d] = send_a[d * 4 + q]

    def forward(src):
        return pltpu.make_async_remote_copy(
            recv_b.at[core, src], recv_b.at[core, src], s_send, s_recv.at[src],
            device_id={"chan": c ^ 1}, device_id_type=MESH,
        )

    def spread(side, src, mine):
        row = pl.multiple_of((src // 2) * 128 + lax.rem(src, 2) * 32 + side * 16, 16)
        for k in range(KB):
            z = recv_b[side, src, k]
            zf = z.astype(F32)
            turned = pltpu.roll(zf, 64, 1) * sign64 if k < DAYS else swap16(zf) * sign16
            far[pl.ds(row, 16), k * 128 : (k + 1) * 128] = z
            far[pl.ds(row + 64, 16), k * 128 : (k + 1) * 128] = turned.astype(BF16)
            if mine:
                near[pl.ds(pl.multiple_of(src * 16, 16), 16), k * 128 : (k + 1) * 128] = z

    for s in range(4):
        q = chip_lo ^ s
        pltpu.make_async_copy(
            recv_a.at[q, pl.ds(0, 7)], recv_a.at[q, pl.ds(0, 7)], a_recv.at[s]
        ).wait()
        for h in range(2):
            tiles = [recv_a[q, 4 * h + n, 64:80, :].astype(F32) for n in range(4)]
            for u in range(4):
                mixed = tiles[u]
                for n in range(4):
                    if n != u:
                        moved = pltpu.roll(tiles[n], (32 * (n - u)) % 128, 1)
                        mixed = jnp.where(group == n, moved, mixed)
                mix_f[pl.ds(h * 64 + u, 16, stride=4), :] = mixed
        for jj in range(4):
            j = chip_hi ^ jj
            to = 4 * j + q
            rows = pl.ds(pl.multiple_of(j * 16, 16), 16)
            tail_rows = [pl.ds(pl.multiple_of(h * 64 + j * 16, 16), 16) for h in range(2)]
            if s == 0 and jj == 0:
                recv_b[core, chip, 0:8] = recv_a[q, :, rows, :]
                for h in range(2):
                    recv_b[core, chip, 8 + h] = mix_f[tail_rows[h], :].astype(BF16)
                forward(chip).start()
            else:
                send_b[to, 0:8] = recv_a[q, :, rows, :]
                for h in range(2):
                    send_b[to, 8 + h] = mix_f[tail_rows[h], :].astype(BF16)
                pltpu.make_async_remote_copy(
                    send_b.at[to], recv_b.at[core, chip], b_send, b_recv.at[chip],
                    device_id={"chan": to * 2 + core}, device_id_type=MESH,
                ).start()

    spread(core, chip, True)

    def at(n):
        return chip ^ (lax.rem(n, 4) * 4 + n // 4)

    def take_other(src):
        side = 1 - core
        pltpu.make_async_copy(recv_b.at[side, src], recv_b.at[side, src], s_recv.at[src]).wait()
        spread(side, src, False)

    def arrive(n, carry):
        src = at(n)
        pltpu.make_async_copy(recv_b.at[core, src], recv_b.at[core, src], b_recv.at[src]).wait()
        forward(src).start()
        spread(core, src, True)
        take_other(at(n - 1))
        return carry

    lax.fori_loop(1, CHIPS, arrive, 0)
    take_other(at(CHIPS - 1))

    for s in range(4):
        p = (d // 2) ^ s
        prod = lax.dot_general(
            near[...], far[pl.ds(pl.multiple_of(p * 256, 256), 256), :], NT,
            preferred_element_type=F32,
        )
        for e in range(2):
            send_c[2 * p + e] = prod[:, e * 128 : (e + 1) * 128].astype(BF16).reshape(CHIPS, 16, 128)

        def keep(day, to):
            pltpu.make_async_remote_copy(
                send_c.at[day, to], recv_d.at[d, chip], d_send, d_recv.at[d],
                device_id={"chan": to * 2 + core, "day": day}, device_id_type=MESH,
            ).start()

        def keep_both(m, carry):
            for e in range(2):
                keep(d ^ (2 * s + e), chip ^ m)
            return carry

        lax.fori_loop(1, CHIPS, keep_both, 0)
        keep(d ^ (2 * s + 1), chip)
        if s == 0:
            recv_d[d, chip] = send_c[d, chip]
        else:
            keep(d ^ (2 * s), chip)

    for e in range(DAYS):
        src = d ^ e
        some = recv_d.at[src] if e else recv_d.at[src, pl.ds(0, 15)]
        pltpu.make_async_copy(some, some, d_recv.at[src]).wait()
        lag_f[pl.ds(pl.multiple_of(src * 256, 256), 256), :] = (
            recv_d[src].reshape(256, 128).astype(F32)
        )

    tables_copy.wait()
    for n in range(4):
        for u in range(4):
            t = lag_f[pl.ds(n * 4 + u, 128, stride=16), :].T.astype(BF16)
            lag_rows[u * 64 : (u + 1) * 64, 0:128] = t[0:64]
            lag_rows[u * 64 : (u + 1) * 64, 128:256] = t[64:128]
        rows = lag_rows[...]
        lags = jnp.dot(rows, tables[0], preferred_element_type=F32)
        lags = lags + jnp.dot(rows, tables[1], preferred_element_type=F32)
        for u in range(4):
            for h in range(2):
                out_f[h, pl.ds(n * 4 + u, 64, stride=16), :] = (
                    lags[u * 64 : (u + 1) * 64, h * 128 : (h + 1) * 128]
                )
    for h in range(2):
        out_ref[:, h * 128 : (h + 1) * 128] = out_f[h]

    sent = send_a.at[pl.ds(0, 28)]
    pltpu.make_async_copy(sent, sent, a_send).wait()
    sent = send_b.at[pl.ds(0, 15)]
    pltpu.make_async_copy(sent, sent, b_send).wait()
    sent = recv_b.at[0]
    pltpu.make_async_copy(sent, sent, s_send).wait()
    sent = send_c.reshape(128, 16, 128).at[pl.ds(0, 127)]
    pltpu.make_async_copy(sent, sent, d_send).wait()


def shards(spectra):
    dma = pltpu.SemaphoreType.DMA
    out = pl.pallas_call(
        kernel,
        out_shape=jax.ShapeDtypeStruct((1024, 256), F32),
        in_specs=[pl.BlockSpec(memory_space=pltpu.HBM)] * 3,
        out_specs=pl.BlockSpec(memory_space=pltpu.VMEM),
        scratch_shapes=[
            pltpu.VMEM((CH, WINDOWS, 2 * BINS), BF16),
            pltpu.VMEM((BINS, 128), F32),
            pltpu.VMEM((2, LAGS, LAGS), BF16),
            pltpu.VMEM((2048, 128), F32),
            pltpu.VMEM((512, 128), F32),
            pltpu.VMEM((32, 80, 128), BF16),
            pltpu.VMEM((4, 8, 80, 128), BF16),
            pltpu.VMEM((128, 128), F32),
            pltpu.VMEM((CHIPS, KB, 16, 128), BF16),
            pltpu.VMEM((2, CHIPS, KB, 16, 128), BF16),
            pltpu.VMEM((256, KB * 128), BF16),
            pltpu.VMEM((1024, KB * 128), BF16),
            pltpu.VMEM((DAYS, CHIPS, 16, 128), BF16),
            pltpu.VMEM((DAYS, CHIPS, 16, 128), BF16),
            pltpu.VMEM((2048, 128), F32),
            pltpu.VMEM((256, 256), BF16),
            pltpu.VMEM((2, 1024, 128), F32),
            dma((4,)),
            dma,
            dma,
            dma,
            dma((4,)),
            dma,
            dma((CHIPS,)),
            dma,
            dma((CHIPS,)),
            dma,
            dma((DAYS,)),
        ],
        compiler_params=pltpu.CompilerParams(
            collective_id=0, has_side_effects=True, vmem_limit_bytes=56 << 20
        ),
    )(spectra, jnp.asarray(taper_table()), jnp.asarray(np.stack(lag_tables())))
    return out.reshape(64, 16, 256)


def solution(mesh):
    return jax.shard_map(
        shards,
        mesh=mesh,
        in_specs=(P("day", "chan", None, None),),
        out_specs=P("day", "chan", None),
        check_vma=False,
    )
```

```python
import jax
import jax.numpy as jnp
import numpy as np
from jax import lax
from jax.experimental import pallas as pl
from jax.experimental.pallas import tpu as pltpu
from jax.sharding import PartitionSpec as P

F32 = jnp.float32
BF16 = jnp.bfloat16
MESH = pl.DeviceIdType.MESH
BINS = 128
LAGS = 256
WINDOWS = 80
CH = 16
DAYS = 8
CHIPS = 16
HEAD = 64
KB = 10
NT = (((1,), (1,)), ((), ()))


def taper_table():
    f = np.arange(BINS, dtype=np.float64)
    taper = 0.54 - 0.46 * np.cos(2.0 * np.pi * (f + 0.5) / BINS)
    return np.ascontiguousarray(np.broadcast_to(taper[:, None], (BINS, 128)).astype(np.float32))


def lag_tables():
    slot = np.arange(BINS)
    day = slot // CHIPS
    f = (day % 4) * 32 + (day // 4) * 16 + slot % CHIPS
    wound = (f[:, None] * (np.arange(LAGS)[None, :] - BINS)) % LAGS
    angle = 2.0 * np.pi / LAGS * wound
    table = np.concatenate([np.cos(angle), -np.sin(angle)], axis=0) / (WINDOWS * DAYS)
    table = table.astype(np.float32)
    high = table.astype(jnp.bfloat16)
    low = (table - high.astype(np.float32)).astype(jnp.bfloat16)
    return high, low


def kernel(
    x_hbm, taper_hbm, tables_hbm, out_ref,
    x_ref, taper_ref, tables, head_f, send_m, send_t, recv_t, mix_f, send_e, recv_m, far,
    send_c, recv_d, lag_f, lag_rows, out_f,
    x_in, taper_in, tables_in,
    ready, t_send, t_recv, m_send, m_recv, e_send, f_send, f_recv, d_send, d_recv,
):
    c = lax.axis_index("chan")
    d = lax.axis_index("day")
    core = lax.rem(c, 2)
    chip = c // 2
    x = lax.rem(d, 4)
    y = d // 4

    x_copies = [
        pltpu.make_async_copy(
            x_hbm.at[0, pl.ds(4 * g, 4)], x_ref.at[pl.ds(4 * g, 4)], x_in.at[g]
        )
        for g in range(4)
    ]
    taper_copy = pltpu.make_async_copy(taper_hbm, taper_ref, taper_in)
    tables_copy = pltpu.make_async_copy(tables_hbm, tables, tables_in)
    x_copies[0].start()
    taper_copy.start()
    for g in range(1, 4):
        x_copies[g].start()
    tables_copy.start()

    barrier = pltpu.get_barrier_semaphore()
    for e in range(1, DAYS):
        pl.semaphore_signal(barrier, inc=1, device_id={"day": d ^ e}, device_id_type=MESH)
    for m in range(1, CHIPS):
        pl.semaphore_signal(barrier, inc=1, device_id={"chan": c ^ (2 * m)}, device_id_type=MESH)
    pl.semaphore_signal(barrier, inc=1, device_id={"chan": c ^ 1}, device_id_type=MESH)

    lane = lax.broadcasted_iota(jnp.int32, (1, 128), 1)
    group = lane // 32
    first16 = lax.rem(lane, 32) < 16
    sign64 = jnp.where(lane < 64, -1.0, 1.0).astype(F32)
    sign16 = jnp.where(first16, -1.0, 1.0).astype(F32)

    def swap16(v):
        return jnp.where(first16, pltpu.roll(v, 112, 1), pltpu.roll(v, 16, 1))

    def whiten(rows, partner):
        t = jnp.concatenate(rows, axis=0).T
        part = jnp.sum(t * t, axis=0, keepdims=True)
        power = (part + partner(part)) / BINS + 1e-06
        return t * taper_ref[...] * (1.0 / jnp.sqrt(power))

    taper_copy.wait()
    for g in range(4):
        x_copies[g].wait()
        rows = []
        for u in range(4):
            v = x_ref[4 * g + u, HEAD:, :].astype(F32)
            rows += [v[:, :128], v[:, 128:]]
        t = whiten(rows, swap16).astype(BF16)
        for n in range(4):
            send_t[n, g] = t[32 * n : 32 * n + 32]

    def whiten_heads(g, carry):
        for u in range(4):
            v = x_ref[4 * g + u, :HEAD, :].astype(F32)
            t = whiten([v[:, :128], v[:, 128:]], lambda part: pltpu.roll(part, 64, 1))
            head_f[pl.ds(4 * g + u, 128, stride=CH), :] = t
        return carry

    lax.fori_loop(0, 4, whiten_heads, 0)

    def pack(b, carry):
        part = head_f[pl.ds(pl.multiple_of(b * 128, 128), 128), :].astype(BF16)
        send_m[pl.ds(b * 8, 8)] = part.reshape(8, 16, 128)
        return carry

    lax.fori_loop(0, 16, pack, 0)

    pl.semaphore_wait(barrier, 23)
    for e in range(1, DAYS):
        pl.semaphore_signal(ready, inc=1, device_id={"day": d ^ e}, device_id_type=MESH)
    for n in range(1, 4):
        pltpu.make_async_remote_copy(
            send_t.at[x ^ n], recv_t.at[x], t_send, t_recv,
            device_id={"day": d ^ n}, device_id_type=MESH,
        ).start()
    recv_t[x] = send_t[x]

    pl.semaphore_wait(ready, 7)

    order = (0, 4, 1, 5, 2, 6, 3, 7)
    for e in order:
        to_day = d ^ e
        slot = lax.rem(to_day, 4) * 32 + (to_day // 4) * 16

        def send_head(m, carry, e=e, to_day=to_day, slot=slot):
            to = chip ^ m
            pltpu.make_async_remote_copy(
                send_m.at[slot + to], recv_m.at[core, d, chip], m_send, m_recv.at[e],
                device_id={"chan": to * 2 + core, "day": to_day}, device_id_type=MESH,
            ).start()
            return carry

        lax.fori_loop(1 if e == 0 else 0, CHIPS, send_head, 0)
    recv_m[core, d, chip] = send_m[x * 32 + y * 16 + chip]

    pltpu.make_async_copy(recv_t.at[pl.ds(0, 3)], recv_t.at[pl.ds(0, 3)], t_recv).wait()
    for g in range(4):
        tiles = [recv_t[n, g].astype(F32) for n in range(4)]
        for u in range(4):
            mixed = tiles[u]
            for n in range(4):
                if n != u:
                    mixed = jnp.where(group == n, pltpu.roll(tiles[n], (32 * (n - u)) % 128, 1), mixed)
            mix_f[pl.ds(4 * g + u, 32, stride=CH), :] = mixed
    send_e[...] = mix_f[...].astype(BF16).reshape(32, 16, 128)
    for h in range(2):
        to_day = d ^ (4 * h)
        slot = (y ^ h) * 16

        def send_tail(m, carry, h=h, to_day=to_day, slot=slot):
            to = chip ^ m
            pltpu.make_async_remote_copy(
                send_e.at[slot + to], recv_m.at[core, DAYS + y, chip], e_send, m_recv.at[DAYS + h],
                device_id={"chan": to * 2 + core, "day": to_day}, device_id_type=MESH,
            ).start()
            return carry

        lax.fori_loop(1 if h == 0 else 0, CHIPS, send_tail, 0)
    recv_m[core, DAYS + y, chip] = send_e[y * 16 + chip]

    def spread(side, k, tail):
        z = recv_m[side, k].reshape(256, 128)
        zf = z.astype(F32)
        turned = swap16(zf) * sign16 if tail else pltpu.roll(zf, 64, 1) * sign64
        turned = turned.astype(BF16)
        for n in range(DAYS):
            row = pl.multiple_of(n * 128 + side * 32, 32)
            far[k, pl.ds(row, 32), :] = z[32 * n : 32 * n + 32]
            far[k, pl.ds(row + 64, 32), :] = turned[32 * n : 32 * n + 32]

    blocks = [(e, d ^ e) for e in order] + [(DAYS + h, DAYS + (y ^ h)) for h in range(2)]

    def take_other(i, k):
        some = recv_m.at[1 - core, k]
        pltpu.make_async_copy(some, some, f_recv.at[i]).wait()
        spread(1 - core, k, i >= DAYS)

    last = None
    for i, k in blocks:
        some = recv_m.at[core, k]
        part = recv_m.at[core, k, pl.ds(0, 15)] if i in (0, DAYS) else some
        pltpu.make_async_copy(part, part, m_recv.at[i]).wait()
        pltpu.make_async_remote_copy(
            some, some, f_send, f_recv.at[i], device_id={"chan": c ^ 1}, device_id_type=MESH,
        ).start()
        spread(core, k, i >= DAYS)
        if last is not None:
            take_other(*last)
        last = (i, k)
    take_other(*last)

    near = jnp.concatenate([recv_m[core, k].reshape(256, 128) for k in range(KB)], axis=1)

    for s in range(4):
        p = (d // 2) ^ s
        rows = pl.ds(pl.multiple_of(p * 256, 256), 256)
        prod = lax.dot_general(
            near, jnp.concatenate([far[k, rows, :] for k in range(KB)], axis=1), NT,
            preferred_element_type=F32,
        )
        for e in range(2):
            send_c[2 * p + e] = prod[:, e * 128 : (e + 1) * 128].astype(BF16).reshape(CHIPS, 16, 128)

        def keep(day, to):
            pltpu.make_async_remote_copy(
                send_c.at[day, to], recv_d.at[d, chip], d_send, d_recv.at[d],
                device_id={"chan": to * 2 + core, "day": day}, device_id_type=MESH,
            ).start()

        def keep_both(m, carry):
            for e in range(2):
                keep(d ^ (2 * s + e), chip ^ m)
            return carry

        lax.fori_loop(1, CHIPS, keep_both, 0)
        keep(d ^ (2 * s + 1), chip)
        if s == 0:
            recv_d[d, chip] = send_c[d, chip]
        else:
            keep(d ^ (2 * s), chip)

    for e in range(DAYS):
        src = d ^ e
        some = recv_d.at[src] if e else recv_d.at[src, pl.ds(0, 15)]
        pltpu.make_async_copy(some, some, d_recv.at[src]).wait()
        lag_f[pl.ds(pl.multiple_of(src * 256, 256), 256), :] = (
            recv_d[src].reshape(256, 128).astype(F32)
        )

    tables_copy.wait()
    for n in range(4):
        for u in range(4):
            t = lag_f[pl.ds(n * 4 + u, 128, stride=16), :].T.astype(BF16)
            lag_rows[u * 64 : (u + 1) * 64, 0:128] = t[0:64]
            lag_rows[u * 64 : (u + 1) * 64, 128:256] = t[64:128]
        rows = lag_rows[...]
        lags = jnp.dot(rows, tables[0], preferred_element_type=F32)
        lags = lags + jnp.dot(rows, tables[1], preferred_element_type=F32)
        for u in range(4):
            for side in range(2):
                for b in range(2):
                    src = u * 64 + side * 32 + b * 16
                    dst = (b * 32 + side * 16) * 16 + n * 4 + u
                    for h in range(2):
                        out_f[h, pl.ds(dst, 16, stride=16), :] = (
                            lags[src : src + 16, h * 128 : (h + 1) * 128]
                        )
    for h in range(2):
        out_ref[:, h * 128 : (h + 1) * 128] = out_f[h]

    sent = send_t.at[pl.ds(0, 3)]
    pltpu.make_async_copy(sent, sent, t_send).wait()
    sent = send_m.at[pl.ds(0, 127)]
    pltpu.make_async_copy(sent, sent, m_send).wait()
    sent = send_e.at[pl.ds(0, 31)]
    pltpu.make_async_copy(sent, sent, e_send).wait()
    sent = recv_m.at[0]
    pltpu.make_async_copy(sent, sent, f_send).wait()
    sent = send_m.at[pl.ds(0, 127)]
    pltpu.make_async_copy(sent, sent, d_send).wait()


def shards(spectra):
    dma = pltpu.SemaphoreType.DMA
    out = pl.pallas_call(
        kernel,
        out_shape=jax.ShapeDtypeStruct((1024, 256), F32),
        in_specs=[pl.BlockSpec(memory_space=pltpu.HBM)] * 3,
        out_specs=pl.BlockSpec(memory_space=pltpu.VMEM),
        scratch_shapes=[
            pltpu.VMEM((CH, WINDOWS, 2 * BINS), BF16),
            pltpu.VMEM((BINS, 128), F32),
            pltpu.VMEM((2, LAGS, LAGS), BF16),
            pltpu.VMEM((2048, 128), F32),
            pltpu.VMEM((BINS, 16, 128), BF16),
            pltpu.VMEM((4, 4, 32, 128), BF16),
            pltpu.VMEM((4, 4, 32, 128), BF16),
            pltpu.VMEM((512, 128), F32),
            pltpu.VMEM((32, 16, 128), BF16),
            pltpu.VMEM((2, KB, CHIPS, 16, 128), BF16),
            pltpu.VMEM((KB, 1024, 128), BF16),
            pltpu.VMEM((DAYS, CHIPS, 16, 128), BF16),
            pltpu.VMEM((DAYS, CHIPS, 16, 128), BF16),
            pltpu.VMEM((2048, 128), F32),
            pltpu.VMEM((256, 256), BF16),
            pltpu.VMEM((2, 1024, 128), F32),
            dma((4,)),
            dma,
            dma,
            pltpu.SemaphoreType.REGULAR,
            dma,
            dma,
            dma,
            dma((KB,)),
            dma,
            dma,
            dma((KB,)),
            dma,
            dma((DAYS,)),
        ],
        compiler_params=pltpu.CompilerParams(
            collective_id=0, has_side_effects=True, vmem_limit_bytes=40 << 20
        ),
    )(*[
        pltpu.with_memory_space_constraint(v, pltpu.HBM)
        for v in (spectra, jnp.asarray(taper_table()), jnp.asarray(np.stack(lag_tables())))
    ])
    return out.reshape(64, 16, 256)


def solution(mesh):
    return jax.shard_map(
        shards,
        mesh=mesh,
        in_specs=(P("day", "chan", None, None),),
        out_specs=P("day", "chan", None),
        check_vma=False,
    )
```

```python
import jax
import jax.numpy as jnp
import numpy as np
from jax import lax
from jax.experimental import pallas as pl
from jax.experimental.pallas import tpu as pltpu
from jax.sharding import PartitionSpec as P

F32 = jnp.float32
BF16 = jnp.bfloat16
MESH = pl.DeviceIdType.MESH
BINS = 128
LAGS = 256
WINDOWS = 80
CH = 16
DAYS = 8
CHIPS = 16
HEAD = 64
KB = 10
NT = (((1,), (1,)), ((), ()))


def taper_table():
    f = np.arange(BINS, dtype=np.float64)
    taper = 0.54 - 0.46 * np.cos(2.0 * np.pi * (f + 0.5) / BINS)
    return np.ascontiguousarray(np.broadcast_to(taper[:, None], (BINS, 128)).astype(np.float32))


def lag_tables():
    slot = np.arange(BINS)
    day = slot // CHIPS
    f = (day % 4) * 32 + (day // 4) * 16 + slot % CHIPS
    wound = (f[:, None] * (np.arange(LAGS)[None, :] - BINS)) % LAGS
    angle = 2.0 * np.pi / LAGS * wound
    table = np.concatenate([np.cos(angle), -np.sin(angle)], axis=0) / (WINDOWS * DAYS)
    table = table.astype(np.float32)
    high = table.astype(jnp.bfloat16)
    low = (table - high.astype(np.float32)).astype(jnp.bfloat16)
    return high, low


def kernel(
    x_hbm, taper_hbm, tables_hbm, out_ref,
    x_ref, taper_ref, tables, head_f, send_m, send_t, recv_t, mix_f, send_e, recv_m, far,
    send_c, recv_d, lag_f, lag_rows, out_f,
    x_in, taper_in, tables_in,
    ready, t_send, t_recv, m_send, m_recv, e_send, s_send, d_send, d_recv,
):
    c = lax.axis_index("chan")
    d = lax.axis_index("day")
    core = lax.rem(c, 2)
    z = lax.rem(c // 2, 8)
    y_hi = c // 16
    chip = z * 2 + y_hi
    x = lax.rem(d, 4)
    y = d // 4

    def chan_at(m):
        return c ^ (lax.rem(m, 2) * 16 + (m // 2) * 2)

    barrier = pltpu.get_barrier_semaphore()

    def greet_chan(to):
        pl.semaphore_signal(barrier, inc=1, device_id={"chan": to}, device_id_type=MESH)

    @pl.when(core == 0)
    def _():
        for m in range(CHIPS - 1, 0, -1):
            greet_chan(chan_at(m))
            greet_chan(chan_at(m) + 1)

    greet_chan(c ^ 1)
    for e in range(1, DAYS):
        pl.semaphore_signal(barrier, inc=1, device_id={"day": d ^ e}, device_id_type=MESH)

    x_copies = [
        pltpu.make_async_copy(
            x_hbm.at[0, pl.ds(4 * g, 4)], x_ref.at[pl.ds(4 * g, 4)], x_in.at[g]
        )
        for g in range(4)
    ]
    taper_copy = pltpu.make_async_copy(taper_hbm, taper_ref, taper_in)
    tables_copy = pltpu.make_async_copy(tables_hbm, tables, tables_in)
    x_copies[0].start()
    taper_copy.start()
    for g in range(1, 4):
        x_copies[g].start()
    tables_copy.start()

    lane = lax.broadcasted_iota(jnp.int32, (1, 128), 1)
    group = lane // 32
    first16 = lax.rem(lane, 32) < 16
    sign64 = jnp.where(lane < 64, -1.0, 1.0).astype(F32)
    sign16 = jnp.where(first16, -1.0, 1.0).astype(F32)

    def swap16(v):
        return jnp.where(first16, pltpu.roll(v, 112, 1), pltpu.roll(v, 16, 1))

    def whiten(rows, partner):
        t = jnp.concatenate(rows, axis=0).T
        part = jnp.sum(t * t, axis=0, keepdims=True)
        power = (part + partner(part)) / BINS + 1e-06
        return t * taper_ref[...] * (1.0 / jnp.sqrt(power))

    taper_copy.wait()
    for g in range(4):
        x_copies[g].wait()
        rows = []
        for u in range(4):
            v = x_ref[4 * g + u, HEAD:, :].astype(F32)
            rows += [v[:, :128], v[:, 128:]]
        t = whiten(rows, swap16).astype(BF16)
        for n in range(4):
            send_t[n, g] = t[32 * n : 32 * n + 32]

    def whiten_heads(g, carry):
        for u in range(4):
            v = x_ref[4 * g + u, :HEAD, :].astype(F32)
            t = whiten([v[:, :128], v[:, 128:]], lambda part: pltpu.roll(part, 64, 1))
            head_f[pl.ds(4 * g + u, 128, stride=CH), :] = t
        return carry

    lax.fori_loop(0, 4, whiten_heads, 0)

    def pack(b, carry):
        part = head_f[pl.ds(pl.multiple_of(b * 128, 128), 128), :].astype(BF16)
        send_m[pl.ds(b * 8, 8)] = part.reshape(8, 16, 128)
        return carry

    lax.fori_loop(0, 16, pack, 0)

    pl.semaphore_wait(barrier, 23)
    for e in range(1, DAYS):
        pl.semaphore_signal(ready, inc=1, device_id={"day": d ^ e}, device_id_type=MESH)
    for n in range(1, 4):
        pltpu.make_async_remote_copy(
            send_t.at[x ^ n], recv_t.at[x], t_send, t_recv,
            device_id={"day": d ^ n}, device_id_type=MESH,
        ).start()

    def send_head(e, m, sem):
        day = d ^ e
        slot = lax.rem(day, 4) * 32 + (day // 4) * 16 + (chip ^ m)
        pltpu.make_async_remote_copy(
            send_m.at[slot], recv_m.at[z, core, y_hi, d], m_send, sem,
            device_id={"chan": chan_at(m) - core, "day": day}, device_id_type=MESH,
        ).start()

    def send_same_day(r, carry):
        m = CHIPS - r
        send_head(0, m, m_recv.at[m // 2])
        return carry

    lax.fori_loop(1, CHIPS, send_same_day, 0)
    recv_t[x] = send_t[x]

    def keep_own(src, k):
        @pl.when(core == 0)
        def _():
            recv_m[z, 0, y_hi, k] = src[...]

        @pl.when(core == 1)
        def _():
            pltpu.make_async_remote_copy(
                src, recv_m.at[z, 1, y_hi, k], s_send, m_recv.at[0],
                device_id={"chan": c - 1}, device_id_type=MESH,
            ).start()

    keep_own(send_m.at[x * 32 + y * 16 + chip], d)

    pl.semaphore_wait(ready, 7)

    order = (4, 5, 7, 6, 3, 2, 1, 0)

    def send_heads(mz):
        def send(r, carry):
            send_head(DAYS - r // 2, 2 * mz + lax.rem(r, 2), m_recv.at[mz])
            return carry

        lax.fori_loop(2, 2 * DAYS, send, 0)

    def join_tails():
        pltpu.make_async_copy(recv_t.at[pl.ds(0, 3)], recv_t.at[pl.ds(0, 3)], t_recv).wait()
        for g in range(4):
            tiles = [recv_t[n, g].astype(F32) for n in range(4)]
            for u in range(4):
                mixed = tiles[u]
                for n in range(4):
                    if n != u:
                        moved = pltpu.roll(tiles[n], (32 * (n - u)) % 128, 1)
                        mixed = jnp.where(group == n, moved, mixed)
                mix_f[pl.ds(4 * g + u, 32, stride=CH), :] = mixed
        send_e[...] = mix_f[...].astype(BF16).reshape(32, 16, 128)
        keep_own(send_e.at[y * 16 + chip], DAYS + y)

    def send_tails(mz):
        def send(r, carry):
            h = r // 2
            m = 2 * mz + lax.rem(r, 2)
            pltpu.make_async_remote_copy(
                send_e.at[(y ^ h) * 16 + (chip ^ m)], recv_m.at[z, core, y_hi, DAYS + y],
                e_send, m_recv.at[mz],
                device_id={"chan": chan_at(m) - core, "day": d ^ (4 * h)}, device_id_type=MESH,
            ).start()
            return carry

        lax.fori_loop(0 if mz else 1, 4, send, 0)

    for mz in order[:4]:
        send_heads(mz)
    join_tails()
    for mz in order[:4]:
        send_tails(mz)
    for mz in order[4:]:
        send_heads(mz)
        send_tails(mz)

    def far_rows(p):
        for b in range(2):
            for side in range(2):
                for zz in range(2):
                    tiles = recv_m[lax.rem(p, 2) * 4 + 2 * b + zz, side, p // 2]
                    heads = tiles[:DAYS].reshape(DAYS * 16, 128).astype(F32)
                    tails = tiles[DAYS:].reshape(32, 128).astype(F32)
                    heads = (pltpu.roll(heads, 64, 1) * sign64).astype(BF16)
                    tails = (swap16(tails) * sign16).astype(BF16)
                    row = b * 128 + side * 32 + zz * 16
                    far[:, row : row + 16, :] = tiles
                    far[0:DAYS, row + 64 : row + 80, :] = heads.reshape(DAYS, 16, 128)
                    far[DAYS:KB, row + 64 : row + 80, :] = tails.reshape(2, 16, 128)

    def keep(e, m, side):
        day = d ^ e
        pltpu.make_async_remote_copy(
            send_c.at[day, side, chip ^ m], recv_d.at[d, chip], d_send, d_recv.at[e],
            device_id={"chan": chan_at(m) + side, "day": day}, device_id_type=MESH,
        ).start()

    @pl.when(core == 0)
    def _():
        for mz in order:
            some = recv_m.at[z ^ mz] if mz else send_m.at[pl.ds(0, 38)]
            pltpu.make_async_copy(some, some, m_recv.at[mz]).wait()

        for s in (1, 3, 2, 0):
            p = (d // 2) ^ s
            far_rows(p)
            for side in range(2):
                near = [recv_m[:, side, :, k].reshape(256, 128) for k in range(KB)]
                prod = lax.dot_general(
                    jnp.concatenate(near, axis=1),
                    jnp.concatenate([far[k] for k in range(KB)], axis=1),
                    NT, preferred_element_type=F32,
                ).astype(BF16)
                for b in range(2):
                    send_c[2 * p + b, side] = prod[:, b * 128 : (b + 1) * 128].reshape(CHIPS, 16, 128)

                def keep_all(r, carry, s=s, side=side):
                    keep(2 * s + lax.rem(r, 2), CHIPS - 1 - r // 2, side)
                    return carry

                lax.fori_loop(0, 2 * CHIPS - 2, keep_all, 0)
                keep(2 * s + 1, 0, side)
                if s or side:
                    keep(2 * s, 0, side)
                else:
                    recv_d[d, chip] = send_c[d, 0, chip]

    @pl.when(core == 0)
    def _():
        some = recv_d.at[d, pl.ds(0, 15)]
        pltpu.make_async_copy(some, some, d_recv.at[0]).wait()

    @pl.when(core == 1)
    def _():
        some = recv_d.at[d]
        pltpu.make_async_copy(some, some, d_recv.at[0]).wait()

    for e in range(DAYS):
        src = d ^ e
        if e:
            some = recv_d.at[src]
            pltpu.make_async_copy(some, some, d_recv.at[e]).wait()
        lag_f[pl.ds(pl.multiple_of(src * 256, 256), 256), :] = (
            recv_d[src].reshape(256, 128).astype(F32)
        )

    tables_copy.wait()
    for n in range(4):
        for u in range(4):
            t = lag_f[pl.ds(n * 4 + u, 128, stride=16), :].T.astype(BF16)
            lag_rows[u * 64 : (u + 1) * 64, 0:128] = t[0:64]
            lag_rows[u * 64 : (u + 1) * 64, 128:256] = t[64:128]
        rows = lag_rows[...]
        lags = jnp.dot(rows, tables[0], preferred_element_type=F32)
        lags = lags + jnp.dot(rows, tables[1], preferred_element_type=F32)
        for u in range(4):
            for side in range(2):
                for b in range(2):
                    src = u * 64 + side * 32 + b * 16
                    dst = (b * 32 + side * 16) * 16 + n * 4 + u
                    for h in range(2):
                        out_f[h, pl.ds(dst, 16, stride=16), :] = (
                            lags[src : src + 16, h * 128 : (h + 1) * 128]
                        )
    for h in range(2):
        out_ref[:, h * 128 : (h + 1) * 128] = out_f[h]

    sent = send_t.at[pl.ds(0, 3)]
    pltpu.make_async_copy(sent, sent, t_send).wait()
    sent = send_m.at[pl.ds(0, 127)]
    pltpu.make_async_copy(sent, sent, m_send).wait()
    sent = send_e.at[pl.ds(0, 31)]
    pltpu.make_async_copy(sent, sent, e_send).wait()

    @pl.when(core == 0)
    def _():
        some = send_c.reshape(256, 16, 128).at[pl.ds(0, 255)]
        pltpu.make_async_copy(some, some, d_send).wait()

    @pl.when(core == 1)
    def _():
        some = send_m.at[pl.ds(0, 2)]
        pltpu.make_async_copy(some, some, s_send).wait()


def shards(spectra):
    dma = pltpu.SemaphoreType.DMA
    out = pl.pallas_call(
        kernel,
        out_shape=jax.ShapeDtypeStruct((1024, 256), F32),
        in_specs=[pl.BlockSpec(memory_space=pltpu.HBM)] * 3,
        out_specs=pl.BlockSpec(memory_space=pltpu.VMEM),
        scratch_shapes=[
            pltpu.VMEM((CH, WINDOWS, 2 * BINS), BF16),
            pltpu.VMEM((BINS, 128), F32),
            pltpu.VMEM((2, LAGS, LAGS), BF16),
            pltpu.VMEM((2048, 128), F32),
            pltpu.VMEM((BINS, 16, 128), BF16),
            pltpu.VMEM((4, 4, 32, 128), BF16),
            pltpu.VMEM((4, 4, 32, 128), BF16),
            pltpu.VMEM((512, 128), F32),
            pltpu.VMEM((32, 16, 128), BF16),
            pltpu.VMEM((8, 2, 2, KB, 16, 128), BF16),
            pltpu.VMEM((KB, 256, 128), BF16),
            pltpu.VMEM((DAYS, 2, CHIPS, 16, 128), BF16),
            pltpu.VMEM((DAYS, CHIPS, 16, 128), BF16),
            pltpu.VMEM((2048, 128), F32),
            pltpu.VMEM((256, 256), BF16),
            pltpu.VMEM((2, 1024, 128), F32),
            dma((4,)),
            dma,
            dma,
            pltpu.SemaphoreType.REGULAR,
            dma,
            dma,
            dma,
            dma((8,)),
            dma,
            dma,
            dma,
            dma((DAYS,)),
        ],
        compiler_params=pltpu.CompilerParams(
            collective_id=0, has_side_effects=True, vmem_limit_bytes=40 << 20
        ),
    )(*[
        pltpu.with_memory_space_constraint(v, pltpu.HBM)
        for v in (spectra, jnp.asarray(taper_table()), jnp.asarray(np.stack(lag_tables())))
    ])
    return out.reshape(64, 16, 256)


def solution(mesh):
    return jax.shard_map(
        shards,
        mesh=mesh,
        in_specs=(P("day", "chan", None),),
        out_specs=P("day", "chan"),
        check_vma=False,
    )
```

```python
import jax
import jax.numpy as jnp
import numpy as np
from jax import lax
from jax.experimental import pallas as pl
from jax.experimental.pallas import tpu as pltpu
from jax.sharding import PartitionSpec as P

F32 = jnp.float32
BF16 = jnp.bfloat16
MESH = pl.DeviceIdType.MESH
BINS = 128
LAGS = 256
WINDOWS = 80
CH = 16
DAYS = 8
CHIPS = 16
HEAD = 64
KB = 10
NT = (((1,), (1,)), ((), ()))


def taper_table():
    f = np.arange(BINS, dtype=np.float64)
    taper = 0.54 - 0.46 * np.cos(2.0 * np.pi * (f + 0.5) / BINS)
    return np.ascontiguousarray(np.broadcast_to(taper[:, None], (BINS, 128)).astype(np.float32))


def lag_tables():
    slot = np.arange(BINS)
    day = slot // CHIPS
    f = (day % 4) * 32 + (day // 4) * 16 + slot % CHIPS
    wound = (f[:, None] * (np.arange(LAGS)[None, :] - BINS)) % LAGS
    angle = 2.0 * np.pi / LAGS * wound
    table = np.concatenate([np.cos(angle), -np.sin(angle)], axis=0) / (WINDOWS * DAYS)
    table = table.astype(np.float32)
    high = table.astype(jnp.bfloat16)
    low = (table - high.astype(np.float32)).astype(jnp.bfloat16)
    return high, low


def kernel(
    x_hbm, taper_hbm, tables_hbm, out_ref,
    x_ref, taper_ref, tables, head_f, send_m, send_t, recv_t, mix_f, send_e, recv_m, far,
    send_c, recv_d, lag_f, lag_rows, out_f,
    x_in, taper_in, tables_in,
    ready, t_send, t_recv, m_send, m_recv, e_send, s_send, d_send, d_recv,
):
    c = lax.axis_index("chan")
    d = lax.axis_index("day")
    core = lax.rem(c, 2)
    z = lax.rem(c // 2, 8)
    y_hi = c // 16
    chip = z * 2 + y_hi
    x = lax.rem(d, 4)
    y = d // 4

    def chan_at(m):
        return c ^ (lax.rem(m, 2) * 16 + (m // 2) * 2)

    barrier = pltpu.get_barrier_semaphore()

    def greet_chan(to):
        pl.semaphore_signal(barrier, inc=1, device_id={"chan": to}, device_id_type=MESH)

    @pl.when(core == 0)
    def _():
        for m in range(CHIPS - 1, 0, -1):
            greet_chan(chan_at(m))
            greet_chan(chan_at(m) + 1)

    greet_chan(c ^ 1)
    for e in range(1, DAYS):
        pl.semaphore_signal(barrier, inc=1, device_id={"day": d ^ e}, device_id_type=MESH)

    x_copies = [
        pltpu.make_async_copy(
            x_hbm.at[0, pl.ds(4 * g, 4)], x_ref.at[pl.ds(4 * g, 4)], x_in.at[g]
        )
        for g in range(4)
    ]
    taper_copy = pltpu.make_async_copy(taper_hbm, taper_ref, taper_in)
    tables_copy = pltpu.make_async_copy(tables_hbm, tables, tables_in)
    x_copies[0].start()
    taper_copy.start()
    for g in range(1, 4):
        x_copies[g].start()
    tables_copy.start()

    lane = lax.broadcasted_iota(jnp.int32, (1, 128), 1)
    group = lane // 32
    first16 = lax.rem(lane, 32) < 16
    sign64 = jnp.where(lane < 64, -1.0, 1.0).astype(F32)
    sign16 = jnp.where(first16, -1.0, 1.0).astype(F32)

    def swap16(v):
        return jnp.where(first16, pltpu.roll(v, 112, 1), pltpu.roll(v, 16, 1))

    def whiten(rows, partner):
        t = jnp.concatenate(rows, axis=0).T
        part = jnp.sum(t * t, axis=0, keepdims=True)
        power = (part + partner(part)) / BINS + 1e-06
        return t * taper_ref[...] * (1.0 / jnp.sqrt(power))

    taper_copy.wait()
    for g in range(4):
        x_copies[g].wait()
        rows = []
        for u in range(4):
            v = x_ref[4 * g + u, HEAD:, :].astype(F32)
            rows += [v[:, :128], v[:, 128:]]
        t = whiten(rows, swap16).astype(BF16)
        for n in range(4):
            send_t[n, g] = t[32 * n : 32 * n + 32]

    def whiten_heads(g, carry):
        for u in range(4):
            v = x_ref[4 * g + u, :HEAD, :].astype(F32)
            t = whiten([v[:, :128], v[:, 128:]], lambda part: pltpu.roll(part, 64, 1))
            head_f[pl.ds(4 * g + u, 128, stride=CH), :] = t
        return carry

    lax.fori_loop(0, 4, whiten_heads, 0)

    def pack(b, carry):
        part = head_f[pl.ds(pl.multiple_of(b * 128, 128), 128), :].astype(BF16)
        send_m[pl.ds(b * 8, 8)] = part.reshape(8, 16, 128)
        return carry

    lax.fori_loop(0, 16, pack, 0)

    pl.semaphore_wait(barrier, 23)
    for e in range(1, DAYS):
        pl.semaphore_signal(ready, inc=1, device_id={"day": d ^ e}, device_id_type=MESH)
    for n in range(1, 4):
        pltpu.make_async_remote_copy(
            send_t.at[x ^ n], recv_t.at[x], t_send, t_recv,
            device_id={"day": d ^ n}, device_id_type=MESH,
        ).start()

    def send_head(e, m, sem):
        day = d ^ e
        slot = lax.rem(day, 4) * 32 + (day // 4) * 16 + (chip ^ m)
        pltpu.make_async_remote_copy(
            send_m.at[slot], recv_m.at[z, core, y_hi, d], m_send, sem,
            device_id={"chan": chan_at(m) - core, "day": day}, device_id_type=MESH,
        ).start()

    def send_same_day(r, carry):
        m = CHIPS - r
        send_head(0, m, m_recv.at[m // 2])
        return carry

    lax.fori_loop(1, CHIPS, send_same_day, 0)
    recv_t[x] = send_t[x]

    def keep_own(src, k):
        @pl.when(core == 0)
        def _():
            recv_m[z, 0, y_hi, k] = src[...]

        @pl.when(core == 1)
        def _():
            pltpu.make_async_remote_copy(
                src, recv_m.at[z, 1, y_hi, k], s_send, m_recv.at[0],
                device_id={"chan": c - 1}, device_id_type=MESH,
            ).start()

    keep_own(send_m.at[x * 32 + y * 16 + chip], d)

    pl.semaphore_wait(ready, 7)

    order = (4, 5, 7, 6, 3, 2, 1, 0)

    def send_heads(mz):
        def send(r, carry):
            send_head(DAYS - r // 2, 2 * mz + lax.rem(r, 2), m_recv.at[mz])
            return carry

        lax.fori_loop(2, 2 * DAYS, send, 0)

    def join_tails():
        pltpu.make_async_copy(recv_t.at[pl.ds(0, 3)], recv_t.at[pl.ds(0, 3)], t_recv).wait()
        for g in range(4):
            tiles = [recv_t[n, g].astype(F32) for n in range(4)]
            for u in range(4):
                mixed = tiles[u]
                for n in range(4):
                    if n != u:
                        moved = pltpu.roll(tiles[n], (32 * (n - u)) % 128, 1)
                        mixed = jnp.where(group == n, moved, mixed)
                mix_f[pl.ds(4 * g + u, 32, stride=CH), :] = mixed
        send_e[...] = mix_f[...].astype(BF16).reshape(32, 16, 128)
        keep_own(send_e.at[y * 16 + chip], DAYS + y)

    def send_tails(mz):
        def send(r, carry):
            h = r // 2
            m = 2 * mz + lax.rem(r, 2)
            pltpu.make_async_remote_copy(
                send_e.at[(y ^ h) * 16 + (chip ^ m)], recv_m.at[z, core, y_hi, DAYS + y],
                e_send, m_recv.at[mz],
                device_id={"chan": chan_at(m) - core, "day": d ^ (4 * h)}, device_id_type=MESH,
            ).start()
            return carry

        lax.fori_loop(0 if mz else 1, 4, send, 0)

    def send_day(e):
        def send(r, carry):
            m = CHIPS - 1 - r
            send_head(e, m, m_recv.at[m // 2])
            return carry

        lax.fori_loop(0, CHIPS, send, 0)

    for e in (6, 2, 7, 3):
        send_day(e)
    join_tails()
    for e in (5, 1, 4):
        send_day(e)
    for mz in order:
        send_tails(mz)

    def far_rows(p):
        for b in range(2):
            for side in range(2):
                for zz in range(2):
                    tiles = recv_m[lax.rem(p, 2) * 4 + 2 * b + zz, side, p // 2]
                    heads = tiles[:DAYS].reshape(DAYS * 16, 128).astype(F32)
                    tails = tiles[DAYS:].reshape(32, 128).astype(F32)
                    heads = (pltpu.roll(heads, 64, 1) * sign64).astype(BF16)
                    tails = (swap16(tails) * sign16).astype(BF16)
                    row = b * 128 + side * 32 + zz * 16
                    far[:, row : row + 16, :] = tiles
                    far[0:DAYS, row + 64 : row + 80, :] = heads.reshape(DAYS, 16, 128)
                    far[DAYS:KB, row + 64 : row + 80, :] = tails.reshape(2, 16, 128)

    def keep(e, m, side):
        day = d ^ e
        pltpu.make_async_remote_copy(
            send_c.at[day, side, chip ^ m], recv_d.at[d, chip], d_send, d_recv.at[e],
            device_id={"chan": chan_at(m) + side, "day": day}, device_id_type=MESH,
        ).start()

    @pl.when(core == 0)
    def _():
        for mz in order:
            some = recv_m.at[z ^ mz] if mz else send_m.at[pl.ds(0, 38)]
            pltpu.make_async_copy(some, some, m_recv.at[mz]).wait()

        for s in (1, 3, 2, 0):
            p = (d // 2) ^ s
            far_rows(p)
            for side in (1, 0):
                near = [recv_m[:, side, :, k].reshape(256, 128) for k in range(KB)]
                prod = lax.dot_general(
                    jnp.concatenate(near, axis=1),
                    jnp.concatenate([far[k] for k in range(KB)], axis=1),
                    NT, preferred_element_type=F32,
                ).astype(BF16)
                for b in range(2):
                    send_c[2 * p + b, side] = prod[:, b * 128 : (b + 1) * 128].reshape(CHIPS, 16, 128)

                def keep_all(r, carry, s=s, side=side):
                    keep(2 * s + lax.rem(r, 2), CHIPS - 1 - r // 2, side)
                    return carry

                lax.fori_loop(0, 2 * CHIPS - 2, keep_all, 0)
                keep(2 * s + 1, 0, side)
                if s or side:
                    keep(2 * s, 0, side)
                else:
                    recv_d[d, chip] = send_c[d, 0, chip]

    @pl.when(core == 0)
    def _():
        some = recv_d.at[d, pl.ds(0, 15)]
        pltpu.make_async_copy(some, some, d_recv.at[0]).wait()

    @pl.when(core == 1)
    def _():
        some = recv_d.at[d]
        pltpu.make_async_copy(some, some, d_recv.at[0]).wait()

    for e in range(DAYS):
        src = d ^ e
        if e:
            some = recv_d.at[src]
            pltpu.make_async_copy(some, some, d_recv.at[e]).wait()
        lag_f[pl.ds(pl.multiple_of(src * 256, 256), 256), :] = (
            recv_d[src].reshape(256, 128).astype(F32)
        )

    tables_copy.wait()
    for n in range(4):
        for u in range(4):
            t = lag_f[pl.ds(n * 4 + u, 128, stride=16), :].T.astype(BF16)
            lag_rows[u * 64 : (u + 1) * 64, 0:128] = t[0:64]
            lag_rows[u * 64 : (u + 1) * 64, 128:256] = t[64:128]
        rows = lag_rows[...]
        lags = jnp.dot(rows, tables[0], preferred_element_type=F32)
        lags = lags + jnp.dot(rows, tables[1], preferred_element_type=F32)
        for u in range(4):
            for side in range(2):
                for b in range(2):
                    src = u * 64 + side * 32 + b * 16
                    dst = (b * 32 + side * 16) * 16 + n * 4 + u
                    for h in range(2):
                        out_f[h, pl.ds(dst, 16, stride=16), :] = (
                            lags[src : src + 16, h * 128 : (h + 1) * 128]
                        )
    for h in range(2):
        out_ref[:, h * 128 : (h + 1) * 128] = out_f[h]

    sent = send_t.at[pl.ds(0, 3)]
    pltpu.make_async_copy(sent, sent, t_send).wait()
    sent = send_m.at[pl.ds(0, 127)]
    pltpu.make_async_copy(sent, sent, m_send).wait()
    sent = send_e.at[pl.ds(0, 31)]
    pltpu.make_async_copy(sent, sent, e_send).wait()

    @pl.when(core == 0)
    def _():
        some = send_c.reshape(256, 16, 128).at[pl.ds(0, 255)]
        pltpu.make_async_copy(some, some, d_send).wait()

    @pl.when(core == 1)
    def _():
        some = send_m.at[pl.ds(0, 2)]
        pltpu.make_async_copy(some, some, s_send).wait()


def shards(spectra):
    dma = pltpu.SemaphoreType.DMA
    out = pl.pallas_call(
        kernel,
        out_shape=jax.ShapeDtypeStruct((1024, 256), F32),
        in_specs=[pl.BlockSpec(memory_space=pltpu.HBM)] * 3,
        out_specs=pl.BlockSpec(memory_space=pltpu.VMEM),
        scratch_shapes=[
            pltpu.VMEM((CH, WINDOWS, 2 * BINS), BF16),
            pltpu.VMEM((BINS, 128), F32),
            pltpu.VMEM((2, LAGS, LAGS), BF16),
            pltpu.VMEM((2048, 128), F32),
            pltpu.VMEM((BINS, 16, 128), BF16),
            pltpu.VMEM((4, 4, 32, 128), BF16),
            pltpu.VMEM((4, 4, 32, 128), BF16),
            pltpu.VMEM((512, 128), F32),
            pltpu.VMEM((32, 16, 128), BF16),
            pltpu.VMEM((8, 2, 2, KB, 16, 128), BF16),
            pltpu.VMEM((KB, 256, 128), BF16),
            pltpu.VMEM((DAYS, 2, CHIPS, 16, 128), BF16),
            pltpu.VMEM((DAYS, CHIPS, 16, 128), BF16),
            pltpu.VMEM((2048, 128), F32),
            pltpu.VMEM((256, 256), BF16),
            pltpu.VMEM((2, 1024, 128), F32),
            dma((4,)),
            dma,
            dma,
            pltpu.SemaphoreType.REGULAR,
            dma,
            dma,
            dma,
            dma((8,)),
            dma,
            dma,
            dma,
            dma((DAYS,)),
        ],
        compiler_params=pltpu.CompilerParams(
            collective_id=0, has_side_effects=True, vmem_limit_bytes=40 << 20
        ),
    )(*[
        pltpu.with_memory_space_constraint(v, pltpu.HBM)
        for v in (spectra, jnp.asarray(taper_table()), jnp.asarray(np.stack(lag_tables())))
    ])
    return out.reshape(64, 16, 256)


def solution(mesh):
    return jax.shard_map(
        shards,
        mesh=mesh,
        in_specs=(P("day", "chan", None),),
        out_specs=P("day", "chan"),
        check_vma=False,
    )
```

```python
import jax
import jax.numpy as jnp
import numpy as np
from jax import lax
from jax.experimental import pallas as pl
from jax.experimental.pallas import tpu as pltpu
from jax.sharding import PartitionSpec as P

F32 = jnp.float32
BF16 = jnp.bfloat16
MESH = pl.DeviceIdType.MESH
BINS = 128
LAGS = 256
WINDOWS = 80
CH = 16
DAYS = 8
CHIPS = 16
HEAD = 64
KB = 10
NT = (((1,), (1,)), ((), ()))


def taper_table():
    f = np.arange(BINS, dtype=np.float64)
    taper = 0.54 - 0.46 * np.cos(2.0 * np.pi * (f + 0.5) / BINS)
    return np.ascontiguousarray(np.broadcast_to(taper[:, None], (BINS, 128)).astype(np.float32))


def lag_tables():
    slot = np.arange(BINS)
    day = slot // CHIPS
    f = (day % 4) * 32 + (day // 4) * 16 + slot % CHIPS
    wound = (f[:, None] * (np.arange(LAGS)[None, :] - BINS)) % LAGS
    angle = 2.0 * np.pi / LAGS * wound
    table = np.concatenate([np.cos(angle), -np.sin(angle)], axis=0) / (WINDOWS * DAYS)
    table = table.astype(np.float32)
    high = table.astype(jnp.bfloat16)
    low = (table - high.astype(np.float32)).astype(jnp.bfloat16)
    return high, low


def kernel(
    x_hbm, taper_hbm, tables_hbm, out_ref,
    x_ref, taper_ref, tables, head_f, send_m, send_t, recv_t, mix_f, send_e, recv_m, far,
    send_c, recv_d, lag_f, lag_rows, out_f,
    x_in, taper_in, tables_in,
    ready, t_send, t_recv, m_send, m_recv, e_send, s_send, d_send, d_recv,
):
    c = lax.axis_index("chan")
    d = lax.axis_index("day")
    core = lax.rem(c, 2)
    z = lax.rem(c // 2, 8)
    y_hi = c // 16
    chip = z * 2 + y_hi
    x = lax.rem(d, 4)
    y = d // 4

    def chan_at(m):
        return c ^ (lax.rem(m, 2) * 16 + (m // 2) * 2)

    barrier = pltpu.get_barrier_semaphore()

    def greet_chan(to):
        pl.semaphore_signal(barrier, inc=1, device_id={"chan": to}, device_id_type=MESH)

    @pl.when(core == 0)
    def _():
        for mz in (4, 5, 7, 6, 3, 2, 1):
            greet_chan(chan_at(2 * mz + 1))
            greet_chan(chan_at(2 * mz))
        greet_chan(chan_at(1))

    for e in (6, 2, 7, 3, 5, 1, 4):
        pl.semaphore_signal(barrier, inc=1, device_id={"day": d ^ e}, device_id_type=MESH)

    @pl.when(core == 0)
    def _():
        for mz in (4, 5, 7, 6, 3, 2, 1):
            greet_chan(chan_at(2 * mz + 1) + 1)
            greet_chan(chan_at(2 * mz) + 1)
        greet_chan(chan_at(1) + 1)

    greet_chan(c ^ 1)

    x_copies = [
        pltpu.make_async_copy(
            x_hbm.at[0, pl.ds(4 * g, 4)], x_ref.at[pl.ds(4 * g, 4)], x_in.at[g]
        )
        for g in range(4)
    ]
    taper_copy = pltpu.make_async_copy(taper_hbm, taper_ref, taper_in)
    tables_copy = pltpu.make_async_copy(tables_hbm, tables, tables_in)
    x_copies[0].start()
    taper_copy.start()
    for g in range(1, 4):
        x_copies[g].start()
    tables_copy.start()

    lane = lax.broadcasted_iota(jnp.int32, (1, 128), 1)
    group = lane // 32
    first16 = lax.rem(lane, 32) < 16
    sign64 = jnp.where(lane < 64, -1.0, 1.0).astype(F32)
    sign16 = jnp.where(first16, -1.0, 1.0).astype(F32)

    def swap16(v):
        return jnp.where(first16, pltpu.roll(v, 112, 1), pltpu.roll(v, 16, 1))

    def whiten(rows, partner):
        t = jnp.concatenate(rows, axis=0).T.astype(F32)
        part = jnp.sum(t * t, axis=0, keepdims=True)
        power = (part + partner(part)) / BINS + 1e-06
        return t * taper_ref[...] * (1.0 / jnp.sqrt(power))

    taper_copy.wait()
    for g in range(4):
        x_copies[g].wait()
        rows = []
        for u in range(4):
            v = x_ref[4 * g + u, HEAD:, :]
            rows += [v[:, :128], v[:, 128:]]
        t = whiten(rows, swap16).astype(BF16)
        for n in range(4):
            send_t[n, g] = t[32 * n : 32 * n + 32]

    def whiten_heads(g, carry):
        for u in range(4):
            v = x_ref[4 * g + u, :HEAD, :]
            t = whiten([v[:, :128], v[:, 128:]], lambda part: pltpu.roll(part, 64, 1))
            head_f[pl.ds(4 * g + u, 128, stride=CH), :] = t
        return carry

    lax.fori_loop(0, 4, whiten_heads, 0)

    def pack(b, carry):
        part = head_f[pl.ds(pl.multiple_of(b * 128, 128), 128), :].astype(BF16)
        send_m[pl.ds(b * 8, 8)] = part.reshape(8, 16, 128)
        return carry

    lax.fori_loop(0, 16, pack, 0)

    pl.semaphore_wait(barrier, 23)
    for e in (6, 2, 7, 3, 5, 1, 4):
        pl.semaphore_signal(ready, inc=1, device_id={"day": d ^ e}, device_id_type=MESH)
    for n in (2, 1, 3):
        pltpu.make_async_remote_copy(
            send_t.at[x ^ n], recv_t.at[x], t_send, t_recv,
            device_id={"day": d ^ n}, device_id_type=MESH,
        ).start()

    def send_head(e, m, sem):
        day = d ^ e
        slot = lax.rem(day, 4) * 32 + (day // 4) * 16 + (chip ^ m)
        pltpu.make_async_remote_copy(
            send_m.at[slot], recv_m.at[z, core, y_hi, d], m_send, sem,
            device_id={"chan": chan_at(m) - core, "day": day}, device_id_type=MESH,
        ).start()

    def send_same_day(r, carry):
        m = CHIPS - r
        send_head(0, m, m_recv.at[m // 2])
        return carry

    lax.fori_loop(1, CHIPS, send_same_day, 0)
    recv_t[x] = send_t[x]

    def keep_own(src, k):
        @pl.when(core == 0)
        def _():
            recv_m[z, 0, y_hi, k] = src[...]

        @pl.when(core == 1)
        def _():
            pltpu.make_async_remote_copy(
                src, recv_m.at[z, 1, y_hi, k], s_send, m_recv.at[0],
                device_id={"chan": c - 1}, device_id_type=MESH,
            ).start()

    keep_own(send_m.at[x * 32 + y * 16 + chip], d)

    pl.semaphore_wait(ready, 7)

    order = (4, 5, 7, 6, 3, 2, 1, 0)

    def send_heads(mz):
        def send(r, carry):
            send_head(DAYS - r // 2, 2 * mz + lax.rem(r, 2), m_recv.at[mz])
            return carry

        lax.fori_loop(2, 2 * DAYS, send, 0)

    def join_tails():
        pltpu.make_async_copy(recv_t.at[pl.ds(0, 3)], recv_t.at[pl.ds(0, 3)], t_recv).wait()
        for g in range(4):
            tiles = [recv_t[n, g].astype(F32) for n in range(4)]
            for u in range(4):
                mixed = tiles[u]
                for n in range(4):
                    if n != u:
                        moved = pltpu.roll(tiles[n], (32 * (n - u)) % 128, 1)
                        mixed = jnp.where(group == n, moved, mixed)
                mix_f[pl.ds(4 * g + u, 32, stride=CH), :] = mixed
        send_e[...] = mix_f[...].astype(BF16).reshape(32, 16, 128)
        keep_own(send_e.at[y * 16 + chip], DAYS + y)

    offsets = (4, 3, 5, 2, 6, 1, 7, 0)

    def send_tails(kz):
        mz = lax.rem(z + kz, 8) ^ z

        def send(r, carry):
            h = 1 - r // 2
            m = 2 * mz + 1 - lax.rem(r, 2)
            pltpu.make_async_remote_copy(
                send_e.at[(y ^ h) * 16 + (chip ^ m)], recv_m.at[z, core, y_hi, DAYS + y],
                e_send, m_recv.at[mz],
                device_id={"chan": chan_at(m) - core, "day": d ^ (4 * h)}, device_id_type=MESH,
            ).start()
            return carry

        lax.fori_loop(0, 4 if kz else 3, send, 0)

    def send_day(e):
        def send(r, carry):
            m = CHIPS - 1 - r
            send_head(e, m, m_recv.at[m // 2])
            return carry

        lax.fori_loop(0, CHIPS, send, 0)

    for e in (6, 2, 7, 3):
        send_day(e)
    join_tails()
    for e in (5, 1, 4):
        send_day(e)
    for kz in offsets:
        send_tails(kz)

    def far_rows(p):
        for b in range(2):
            for side in range(2):
                for zz in range(2):
                    tiles = recv_m[lax.rem(p, 2) * 4 + 2 * b + zz, side, p // 2]
                    heads = tiles[:DAYS].reshape(DAYS * 16, 128).astype(F32)
                    tails = tiles[DAYS:].reshape(32, 128).astype(F32)
                    heads = (pltpu.roll(heads, 64, 1) * sign64).astype(BF16)
                    tails = (swap16(tails) * sign16).astype(BF16)
                    row = b * 128 + side * 32 + zz * 16
                    far[:, row : row + 16, :] = tiles
                    far[0:DAYS, row + 64 : row + 80, :] = heads.reshape(DAYS, 16, 128)
                    far[DAYS:KB, row + 64 : row + 80, :] = tails.reshape(2, 16, 128)

    def keep(e, m, side):
        day = d ^ e
        pltpu.make_async_remote_copy(
            send_c.at[day, side, chip ^ m], recv_d.at[d, chip], d_send, d_recv.at[e],
            device_id={"chan": chan_at(m) + side, "day": day}, device_id_type=MESH,
        ).start()

    @pl.when(core == 0)
    def _():
        for mz in order:
            some = recv_m.at[z ^ mz] if mz else send_m.at[pl.ds(0, 38)]
            pltpu.make_async_copy(some, some, m_recv.at[mz]).wait()

        for s in (1, 3, 2, 0):
            p = (d // 2) ^ s
            far_rows(p)
            for side in (1, 0):
                near = [recv_m[:, side, :, k].reshape(256, 128) for k in range(KB)]
                prod = lax.dot_general(
                    jnp.concatenate(near, axis=1),
                    jnp.concatenate([far[k] for k in range(KB)], axis=1),
                    NT, preferred_element_type=F32,
                ).astype(BF16)
                for b in range(2):
                    send_c[2 * p + b, side] = prod[:, b * 128 : (b + 1) * 128].reshape(CHIPS, 16, 128)

                for mh in (1, 0):
                    for kz in offsets:
                        mz = lax.rem(z + kz, 8) ^ z

                        def keep_all(r, carry, s=s, side=side, m=2 * mz + mh):
                            keep(2 * s + 1 - r, m, side)
                            return carry

                        if kz or mh:
                            lax.fori_loop(0, 2, keep_all, 0)
                keep(2 * s + 1, 0, side)
                if s or side:
                    keep(2 * s, 0, side)
                else:
                    recv_d[d, chip] = send_c[d, 0, chip]

    def widen(src):
        lag_f[pl.ds(pl.multiple_of(src * 256, 256), 256), :] = (
            recv_d[src].reshape(256, 128).astype(F32)
        )

    for e in (3, 2, 7, 6, 5, 4, 1):
        some = recv_d.at[d ^ e]
        pltpu.make_async_copy(some, some, d_recv.at[e]).wait()
        widen(d ^ e)

    @pl.when(core == 0)
    def _():
        some = recv_d.at[d, pl.ds(0, 15)]
        pltpu.make_async_copy(some, some, d_recv.at[0]).wait()

    @pl.when(core == 1)
    def _():
        some = recv_d.at[d]
        pltpu.make_async_copy(some, some, d_recv.at[0]).wait()

    widen(d)

    tables_copy.wait()
    for n in range(4):
        for u in range(4):
            t = lag_f[pl.ds(n * 4 + u, 128, stride=16), :].astype(BF16).T
            lag_rows[u * 64 : (u + 1) * 64, 0:128] = t[0:64]
            lag_rows[u * 64 : (u + 1) * 64, 128:256] = t[64:128]
        rows = lag_rows[...]
        lags = jnp.dot(rows, tables[0], preferred_element_type=F32)
        lags = lags + jnp.dot(rows, tables[1], preferred_element_type=F32)
        for u in range(4):
            for side in range(2):
                for b in range(2):
                    src = u * 64 + side * 32 + b * 16
                    dst = (b * 32 + side * 16) * 16 + n * 4 + u
                    for h in range(2):
                        out_f[h, pl.ds(dst, 16, stride=16), :] = (
                            lags[src : src + 16, h * 128 : (h + 1) * 128]
                        )
    for h in range(2):
        out_ref[:, h * 128 : (h + 1) * 128] = out_f[h]

    sent = send_t.at[pl.ds(0, 3)]
    pltpu.make_async_copy(sent, sent, t_send).wait()
    sent = send_m.at[pl.ds(0, 127)]
    pltpu.make_async_copy(sent, sent, m_send).wait()
    sent = send_e.at[pl.ds(0, 31)]
    pltpu.make_async_copy(sent, sent, e_send).wait()

    @pl.when(core == 0)
    def _():
        some = send_c.reshape(256, 16, 128).at[pl.ds(0, 255)]
        pltpu.make_async_copy(some, some, d_send).wait()

    @pl.when(core == 1)
    def _():
        some = send_m.at[pl.ds(0, 2)]
        pltpu.make_async_copy(some, some, s_send).wait()


def shards(spectra):
    dma = pltpu.SemaphoreType.DMA
    out = pl.pallas_call(
        kernel,
        out_shape=jax.ShapeDtypeStruct((1024, 256), F32),
        in_specs=[pl.BlockSpec(memory_space=pltpu.HBM)] * 3,
        out_specs=pl.BlockSpec(memory_space=pltpu.VMEM),
        scratch_shapes=[
            pltpu.VMEM((CH, WINDOWS, 2 * BINS), BF16),
            pltpu.VMEM((BINS, 128), F32),
            pltpu.VMEM((2, LAGS, LAGS), BF16),
            pltpu.VMEM((2048, 128), F32),
            pltpu.VMEM((BINS, 16, 128), BF16),
            pltpu.VMEM((4, 4, 32, 128), BF16),
            pltpu.VMEM((4, 4, 32, 128), BF16),
            pltpu.VMEM((512, 128), F32),
            pltpu.VMEM((32, 16, 128), BF16),
            pltpu.VMEM((8, 2, 2, KB, 16, 128), BF16),
            pltpu.VMEM((KB, 256, 128), BF16),
            pltpu.VMEM((DAYS, 2, CHIPS, 16, 128), BF16),
            pltpu.VMEM((DAYS, CHIPS, 16, 128), BF16),
            pltpu.VMEM((2048, 128), F32),
            pltpu.VMEM((256, 256), BF16),
            pltpu.VMEM((2, 1024, 128), F32),
            dma((4,)),
            dma,
            dma,
            pltpu.SemaphoreType.REGULAR,
            dma,
            dma,
            dma,
            dma((8,)),
            dma,
            dma,
            dma,
            dma((DAYS,)),
        ],
        compiler_params=pltpu.CompilerParams(
            collective_id=0, has_side_effects=True, vmem_limit_bytes=40 << 20
        ),
    )(*[
        pltpu.with_memory_space_constraint(v, pltpu.HBM)
        for v in (spectra, jnp.asarray(taper_table()), jnp.asarray(np.stack(lag_tables())))
    ])
    return out.reshape(64, 16, 256)


def solution(mesh):
    return jax.shard_map(
        shards,
        mesh=mesh,
        in_specs=(P("day", "chan", None),),
        out_specs=P("day", "chan"),
        check_vma=False,
    )
```

```python
import jax
import jax.numpy as jnp
import numpy as np
from jax import lax
from jax.experimental import pallas as pl
from jax.experimental.pallas import tpu as pltpu
from jax.sharding import PartitionSpec as P

F32 = jnp.float32
BF16 = jnp.bfloat16
MESH = pl.DeviceIdType.MESH
BINS = 128
LAGS = 256
WINDOWS = 80
CH = 16
DAYS = 8
CHIPS = 16
HEAD = 64
KB = 10
NT = (((1,), (1,)), ((), ()))


def taper_table():
    f = np.arange(BINS, dtype=np.float64)
    taper = 0.54 - 0.46 * np.cos(2.0 * np.pi * (f + 0.5) / BINS)
    return np.ascontiguousarray(np.broadcast_to(taper[:, None], (BINS, 128)).astype(np.float32))


def lag_tables():
    slot = np.arange(BINS)
    day = slot // CHIPS
    f = (day % 4) * 32 + (day // 4) * 16 + slot % CHIPS
    wound = (f[:, None] * (np.arange(LAGS)[None, :] - BINS)) % LAGS
    angle = 2.0 * np.pi / LAGS * wound
    table = np.concatenate([np.cos(angle), -np.sin(angle)], axis=0) / (WINDOWS * DAYS)
    table = table.astype(np.float32)
    high = table.astype(jnp.bfloat16)
    low = (table - high.astype(np.float32)).astype(jnp.bfloat16)
    return high, low


def kernel(
    x_hbm, taper_hbm, tables_hbm, out_ref,
    x_ref, taper_ref, tables, head_f, send_m, send_t, recv_t, mix_f, send_e, recv_m, far,
    send_c, recv_d, lag_f, lag_rows, out_f,
    x_in, taper_in, tables_in,
    ready, t_send, t_recv, m_send, m_recv, e_send, s_send, d_send, d_recv,
):
    c = lax.axis_index("chan")
    d = lax.axis_index("day")
    core = lax.rem(c, 2)
    z = lax.rem(c // 2, 8)
    y_hi = c // 16
    chip = z * 2 + y_hi
    x = lax.rem(d, 4)
    y = d // 4

    def chan_at(m):
        return c ^ (lax.rem(m, 2) * 16 + (m // 2) * 2)

    barrier = pltpu.get_barrier_semaphore()

    def greet_chan(to):
        pl.semaphore_signal(barrier, inc=1, device_id={"chan": to}, device_id_type=MESH)

    @pl.when(core == 0)
    def _():
        for mz in (4, 5, 7, 6, 3, 2, 1):
            greet_chan(chan_at(2 * mz + 1))
            greet_chan(chan_at(2 * mz))
        greet_chan(chan_at(1))

    for e in (6, 2, 7, 3, 5, 1, 4):
        pl.semaphore_signal(barrier, inc=1, device_id={"day": d ^ e}, device_id_type=MESH)

    @pl.when(core == 0)
    def _():
        for mz in (4, 5, 7, 6, 3, 2, 1):
            greet_chan(chan_at(2 * mz + 1) + 1)
            greet_chan(chan_at(2 * mz) + 1)
        greet_chan(chan_at(1) + 1)

    greet_chan(c ^ 1)

    x_copies = [
        pltpu.make_async_copy(
            x_hbm.at[0, pl.ds(4 * g, 4)], x_ref.at[pl.ds(4 * g, 4)], x_in.at[g]
        )
        for g in range(4)
    ]
    taper_copy = pltpu.make_async_copy(taper_hbm, taper_ref, taper_in)
    tables_copy = pltpu.make_async_copy(tables_hbm, tables, tables_in)
    x_copies[0].start()
    taper_copy.start()
    for g in range(1, 4):
        x_copies[g].start()
    tables_copy.start()

    lane = lax.broadcasted_iota(jnp.int32, (1, 128), 1)
    group = lane // 32
    first16 = lax.rem(lane, 32) < 16
    sign64 = jnp.where(lane < 64, -1.0, 1.0).astype(F32)
    sign16 = jnp.where(first16, -1.0, 1.0).astype(F32)

    def swap16(v):
        return jnp.where(first16, pltpu.roll(v, 112, 1), pltpu.roll(v, 16, 1))

    def whiten(rows, partner):
        t = jnp.concatenate(rows, axis=0).T.astype(F32)
        part = jnp.sum(t * t, axis=0, keepdims=True)
        power = (part + partner(part)) / BINS + 1e-06
        return t * taper_ref[...] * (1.0 / jnp.sqrt(power))

    taper_copy.wait()
    for g in range(4):
        x_copies[g].wait()
        rows = []
        for u in range(4):
            v = x_ref[4 * g + u, HEAD:, :]
            rows += [v[:, :128], v[:, 128:]]
        t = whiten(rows, swap16).astype(BF16)
        for n in range(4):
            send_t[n, g] = t[32 * n : 32 * n + 32]

    def whiten_heads(g, carry):
        for u in range(4):
            v = x_ref[4 * g + u, :HEAD, :]
            t = whiten([v[:, :128], v[:, 128:]], lambda part: pltpu.roll(part, 64, 1))
            head_f[pl.ds(4 * g + u, 128, stride=CH), :] = t
        return carry

    lax.fori_loop(0, 4, whiten_heads, 0)

    def pack(b, carry):
        part = head_f[pl.ds(pl.multiple_of(b * 128, 128), 128), :].astype(BF16)
        send_m[pl.ds(b * 8, 8)] = part.reshape(8, 16, 128)
        return carry

    lax.fori_loop(0, 16, pack, 0)

    pl.semaphore_wait(barrier, 23)
    for e in (6, 2, 7, 3, 5, 1, 4):
        pl.semaphore_signal(ready, inc=1, device_id={"day": d ^ e}, device_id_type=MESH)
    for n in (2, 1, 3):
        pltpu.make_async_remote_copy(
            send_t.at[x ^ n], recv_t.at[x], t_send, t_recv,
            device_id={"day": d ^ n}, device_id_type=MESH,
        ).start()

    def send_head(e, m, sem):
        day = d ^ e
        slot = lax.rem(day, 4) * 32 + (day // 4) * 16 + (chip ^ m)
        pltpu.make_async_remote_copy(
            send_m.at[slot], recv_m.at[z, core, y_hi, d], m_send, sem,
            device_id={"chan": chan_at(m) - core, "day": day}, device_id_type=MESH,
        ).start()

    def send_same_day(r, carry):
        m = CHIPS - r
        send_head(0, m, m_recv.at[m // 2])
        return carry

    lax.fori_loop(1, CHIPS, send_same_day, 0)
    recv_t[x] = send_t[x]

    def keep_own(src, k):
        @pl.when(core == 0)
        def _():
            recv_m[z, 0, y_hi, k] = src[...]

        @pl.when(core == 1)
        def _():
            pltpu.make_async_remote_copy(
                src, recv_m.at[z, 1, y_hi, k], s_send, m_recv.at[0],
                device_id={"chan": c - 1}, device_id_type=MESH,
            ).start()

    keep_own(send_m.at[x * 32 + y * 16 + chip], d)

    pl.semaphore_wait(ready, 7)

    order = (4, 5, 7, 6, 3, 2, 1, 0)

    def send_heads(mz):
        def send(r, carry):
            send_head(DAYS - r // 2, 2 * mz + lax.rem(r, 2), m_recv.at[mz])
            return carry

        lax.fori_loop(2, 2 * DAYS, send, 0)

    def join_tails():
        pltpu.make_async_copy(recv_t.at[pl.ds(0, 3)], recv_t.at[pl.ds(0, 3)], t_recv).wait()
        for g in range(4):
            tiles = [recv_t[n, g].astype(F32) for n in range(4)]
            for u in range(4):
                mixed = tiles[u]
                for n in range(4):
                    if n != u:
                        moved = pltpu.roll(tiles[n], (32 * (n - u)) % 128, 1)
                        mixed = jnp.where(group == n, moved, mixed)
                mix_f[pl.ds(4 * g + u, 32, stride=CH), :] = mixed
        send_e[...] = mix_f[...].astype(BF16).reshape(32, 16, 128)
        keep_own(send_e.at[y * 16 + chip], DAYS + y)

    offsets = (4, 3, 5, 2, 6, 1, 7, 0)

    def send_tails(kz):
        mz = lax.rem(z + kz, 8) ^ z

        def send(r, carry):
            h = 1 - r // 2
            m = 2 * mz + 1 - lax.rem(r, 2)
            pltpu.make_async_remote_copy(
                send_e.at[(y ^ h) * 16 + (chip ^ m)], recv_m.at[z, core, y_hi, DAYS + y],
                e_send, m_recv.at[mz],
                device_id={"chan": chan_at(m) - core, "day": d ^ (4 * h)}, device_id_type=MESH,
            ).start()
            return carry

        lax.fori_loop(0, 4 if kz else 3, send, 0)

    def send_day(e):
        for mh in (1, 0):
            for kz in offsets:
                send_head(e, 2 * (lax.rem(z + kz, 8) ^ z) + mh, m_recv.at[lax.rem(z + kz, 8) ^ z])

    for e in (6, 2, 7, 3):
        send_day(e)
    join_tails()
    for e in (5, 1, 4):
        send_day(e)
    for kz in offsets:
        send_tails(kz)

    def far_rows(p):
        for b in range(2):
            for side in range(2):
                for zz in range(2):
                    tiles = recv_m[lax.rem(p, 2) * 4 + 2 * b + zz, side, p // 2]
                    heads = tiles[:DAYS].reshape(DAYS * 16, 128).astype(F32)
                    tails = tiles[DAYS:].reshape(32, 128).astype(F32)
                    heads = (pltpu.roll(heads, 64, 1) * sign64).astype(BF16)
                    tails = (swap16(tails) * sign16).astype(BF16)
                    row = b * 128 + side * 32 + zz * 16
                    far[:, row : row + 16, :] = tiles
                    far[0:DAYS, row + 64 : row + 80, :] = heads.reshape(DAYS, 16, 128)
                    far[DAYS:KB, row + 64 : row + 80, :] = tails.reshape(2, 16, 128)

    def keep(e, m, side):
        day = d ^ e
        pltpu.make_async_remote_copy(
            send_c.at[day, side, chip ^ m], recv_d.at[d, chip], d_send, d_recv.at[e],
            device_id={"chan": chan_at(m) + side, "day": day}, device_id_type=MESH,
        ).start()

    @pl.when(core == 0)
    def _():
        for mz in order:
            some = recv_m.at[z ^ mz] if mz else send_m.at[pl.ds(0, 38)]
            pltpu.make_async_copy(some, some, m_recv.at[mz]).wait()

        for s in (1, 3, 2, 0):
            p = (d // 2) ^ s
            far_rows(p)
            for side in (1, 0):
                near = [recv_m[:, side, :, k].reshape(256, 128) for k in range(KB)]
                prod = lax.dot_general(
                    jnp.concatenate(near, axis=1),
                    jnp.concatenate([far[k] for k in range(KB)], axis=1),
                    NT, preferred_element_type=F32,
                ).astype(BF16)
                for b in range(2):
                    send_c[2 * p + b, side] = prod[:, b * 128 : (b + 1) * 128].reshape(CHIPS, 16, 128)

                for mh in (1, 0):
                    for kz in offsets:
                        mz = lax.rem(z + kz, 8) ^ z

                        def keep_all(r, carry, s=s, side=side, m=2 * mz + mh):
                            keep(2 * s + 1 - r, m, side)
                            return carry

                        if kz or mh:
                            lax.fori_loop(0, 2, keep_all, 0)
                keep(2 * s + 1, 0, side)
                if s or side:
                    keep(2 * s, 0, side)
                else:
                    recv_d[d, chip] = send_c[d, 0, chip]

    def widen(src):
        lag_f[pl.ds(pl.multiple_of(src * 256, 256), 256), :] = (
            recv_d[src].reshape(256, 128).astype(F32)
        )

    for e in (3, 2, 7, 6, 5, 4, 1):
        some = recv_d.at[d ^ e]
        pltpu.make_async_copy(some, some, d_recv.at[e]).wait()
        widen(d ^ e)

    @pl.when(core == 0)
    def _():
        some = recv_d.at[d, pl.ds(0, 15)]
        pltpu.make_async_copy(some, some, d_recv.at[0]).wait()

    @pl.when(core == 1)
    def _():
        some = recv_d.at[d]
        pltpu.make_async_copy(some, some, d_recv.at[0]).wait()

    widen(d)

    tables_copy.wait()
    for n in range(4):
        for u in range(4):
            t = lag_f[pl.ds(n * 4 + u, 128, stride=16), :].astype(BF16).T
            lag_rows[u * 64 : (u + 1) * 64, 0:128] = t[0:64]
            lag_rows[u * 64 : (u + 1) * 64, 128:256] = t[64:128]
        rows = lag_rows[...]
        lags = jnp.dot(rows, tables[0], preferred_element_type=F32)
        lags = lags + jnp.dot(rows, tables[1], preferred_element_type=F32)
        for u in range(4):
            for side in range(2):
                for b in range(2):
                    src = u * 64 + side * 32 + b * 16
                    dst = (b * 32 + side * 16) * 16 + n * 4 + u
                    for h in range(2):
                        out_f[h, pl.ds(dst, 16, stride=16), :] = (
                            lags[src : src + 16, h * 128 : (h + 1) * 128]
                        )
    for h in range(2):
        out_ref[:, h * 128 : (h + 1) * 128] = out_f[h]

    sent = send_t.at[pl.ds(0, 3)]
    pltpu.make_async_copy(sent, sent, t_send).wait()
    sent = send_m.at[pl.ds(0, 127)]
    pltpu.make_async_copy(sent, sent, m_send).wait()
    sent = send_e.at[pl.ds(0, 31)]
    pltpu.make_async_copy(sent, sent, e_send).wait()

    @pl.when(core == 0)
    def _():
        some = send_c.reshape(256, 16, 128).at[pl.ds(0, 255)]
        pltpu.make_async_copy(some, some, d_send).wait()

    @pl.when(core == 1)
    def _():
        some = send_m.at[pl.ds(0, 2)]
        pltpu.make_async_copy(some, some, s_send).wait()


def shards(spectra):
    dma = pltpu.SemaphoreType.DMA
    out = pl.pallas_call(
        kernel,
        out_shape=jax.ShapeDtypeStruct((1024, 256), F32),
        in_specs=[pl.BlockSpec(memory_space=pltpu.HBM)] * 3,
        out_specs=pl.BlockSpec(memory_space=pltpu.VMEM),
        scratch_shapes=[
            pltpu.VMEM((CH, WINDOWS, 2 * BINS), BF16),
            pltpu.VMEM((BINS, 128), F32),
            pltpu.VMEM((2, LAGS, LAGS), BF16),
            pltpu.VMEM((2048, 128), F32),
            pltpu.VMEM((BINS, 16, 128), BF16),
            pltpu.VMEM((4, 4, 32, 128), BF16),
            pltpu.VMEM((4, 4, 32, 128), BF16),
            pltpu.VMEM((512, 128), F32),
            pltpu.VMEM((32, 16, 128), BF16),
            pltpu.VMEM((8, 2, 2, KB, 16, 128), BF16),
            pltpu.VMEM((KB, 256, 128), BF16),
            pltpu.VMEM((DAYS, 2, CHIPS, 16, 128), BF16),
            pltpu.VMEM((DAYS, CHIPS, 16, 128), BF16),
            pltpu.VMEM((2048, 128), F32),
            pltpu.VMEM((256, 256), BF16),
            pltpu.VMEM((2, 1024, 128), F32),
            dma((4,)),
            dma,
            dma,
            pltpu.SemaphoreType.REGULAR,
            dma,
            dma,
            dma,
            dma((8,)),
            dma,
            dma,
            dma,
            dma((DAYS,)),
        ],
        compiler_params=pltpu.CompilerParams(
            collective_id=0, has_side_effects=True, vmem_limit_bytes=40 << 20
        ),
    )(*[
        pltpu.with_memory_space_constraint(v, pltpu.HBM)
        for v in (spectra, jnp.asarray(taper_table()), jnp.asarray(np.stack(lag_tables())))
    ])
    return out.reshape(64, 16, 256)


def solution(mesh):
    return jax.shard_map(
        shards,
        mesh=mesh,
        in_specs=(P("day", "chan", None),),
        out_specs=P("day", "chan"),
        check_vma=False,
    )
```

```python
import jax
import jax.numpy as jnp
import numpy as np
from jax import lax
from jax.experimental import pallas as pl
from jax.experimental.pallas import tpu as pltpu
from jax.sharding import PartitionSpec as P

F32 = jnp.float32
BF16 = jnp.bfloat16
MESH = pl.DeviceIdType.MESH
BINS = 128
LAGS = 256
WINDOWS = 80
CH = 16
DAYS = 8
CHIPS = 16
HEAD = 64
KB = 10
NT = (((1,), (1,)), ((), ()))


def taper_table():
    f = np.arange(BINS, dtype=np.float64)
    taper = 0.54 - 0.46 * np.cos(2.0 * np.pi * (f + 0.5) / BINS)
    return np.ascontiguousarray(np.broadcast_to(taper[:, None], (BINS, 128)).astype(np.float32))


def lag_tables():
    slot = np.arange(BINS)
    day = slot // CHIPS
    f = (day % 4) * 32 + (day // 4) * 16 + slot % CHIPS
    wound = (f[:, None] * (np.arange(LAGS)[None, :] - BINS)) % LAGS
    angle = 2.0 * np.pi / LAGS * wound
    table = np.concatenate([np.cos(angle), -np.sin(angle)], axis=0) / (WINDOWS * DAYS)
    table = table.astype(np.float32)
    high = table.astype(jnp.bfloat16)
    low = (table - high.astype(np.float32)).astype(jnp.bfloat16)
    return high, low


def kernel(
    x_hbm, taper_hbm, tables_hbm, out_ref,
    x_ref, taper_ref, tables, head_f, send_m, send_t, recv_t, mix_f, send_e, recv_m, far,
    send_c, recv_d, lag_f, lag_rows, out_f,
    x_in, taper_in, tables_in,
    ready, t_send, t_recv, m_send, m_recv, e_send, s_send, d_send, d_recv,
):
    c = lax.axis_index("chan")
    d = lax.axis_index("day")
    core = lax.rem(c, 2)
    z = lax.rem(c // 2, 8)
    y_hi = c // 16
    chip = z * 2 + y_hi
    x = lax.rem(d, 4)
    y = d // 4

    def chan_at(m):
        return c ^ (lax.rem(m, 2) * 16 + (m // 2) * 2)

    barrier = pltpu.get_barrier_semaphore()

    def greet_chan(to):
        pl.semaphore_signal(barrier, inc=1, device_id={"chan": to}, device_id_type=MESH)

    @pl.when(core == 0)
    def _():
        for mz in (4, 5, 7, 6, 3, 2, 1):
            greet_chan(chan_at(2 * mz + 1))
            greet_chan(chan_at(2 * mz))
        greet_chan(chan_at(1))

    for e in (6, 2, 7, 3, 5, 1, 4):
        pl.semaphore_signal(barrier, inc=1, device_id={"day": d ^ e}, device_id_type=MESH)

    @pl.when(core == 0)
    def _():
        for mz in (4, 5, 7, 6, 3, 2, 1):
            greet_chan(chan_at(2 * mz + 1) + 1)
            greet_chan(chan_at(2 * mz) + 1)
        greet_chan(chan_at(1) + 1)

    greet_chan(c ^ 1)

    x_copies = [
        pltpu.make_async_copy(
            x_hbm.at[0, pl.ds(4 * g, 4)], x_ref.at[pl.ds(4 * g, 4)], x_in.at[g]
        )
        for g in range(4)
    ]
    taper_copy = pltpu.make_async_copy(taper_hbm, taper_ref, taper_in)
    tables_copy = pltpu.make_async_copy(tables_hbm, tables, tables_in)
    x_copies[0].start()
    taper_copy.start()
    for g in range(1, 4):
        x_copies[g].start()
    tables_copy.start()

    lane = lax.broadcasted_iota(jnp.int32, (1, 128), 1)
    group = lane // 32
    first16 = lax.rem(lane, 32) < 16
    sign64 = jnp.where(lane < 64, -1.0, 1.0).astype(F32)
    sign16 = jnp.where(first16, -1.0, 1.0).astype(F32)

    def swap16(v):
        return jnp.where(first16, pltpu.roll(v, 112, 1), pltpu.roll(v, 16, 1))

    def whiten(rows, partner):
        t = jnp.concatenate(rows, axis=0).T.astype(F32)
        part = jnp.sum(t * t, axis=0, keepdims=True)
        power = (part + partner(part)) / BINS + 1e-06
        return t * taper_ref[...] * (1.0 / jnp.sqrt(power))

    taper_copy.wait()
    for g in range(4):
        x_copies[g].wait()
        rows = []
        for u in range(4):
            v = x_ref[4 * g + u, HEAD:, :]
            rows += [v[:, :128], v[:, 128:]]
        t = whiten(rows, swap16).astype(BF16)
        for n in range(4):
            send_t[n, g] = t[32 * n : 32 * n + 32]

    def whiten_heads(g, carry):
        for u in range(4):
            v = x_ref[4 * g + u, :HEAD, :]
            t = whiten([v[:, :128], v[:, 128:]], lambda part: pltpu.roll(part, 64, 1))
            head_f[pl.ds(4 * g + u, 128, stride=CH), :] = t
        return carry

    lax.fori_loop(0, 4, whiten_heads, 0)

    def pack(b, carry):
        part = head_f[pl.ds(pl.multiple_of(b * 128, 128), 128), :].astype(BF16)
        send_m[pl.ds(b * 8, 8)] = part.reshape(8, 16, 128)
        return carry

    lax.fori_loop(0, 16, pack, 0)

    pl.semaphore_wait(barrier, 23)
    for e in (6, 2, 7, 3, 5, 1, 4):
        pl.semaphore_signal(ready, inc=1, device_id={"day": d ^ e}, device_id_type=MESH)
    for n in (2, 1, 3):
        pltpu.make_async_remote_copy(
            send_t.at[x ^ n], recv_t.at[x], t_send, t_recv,
            device_id={"day": d ^ n}, device_id_type=MESH,
        ).start()

    def send_head(e, m, sem):
        day = d ^ e
        slot = lax.rem(day, 4) * 32 + (day // 4) * 16 + (chip ^ m)
        pltpu.make_async_remote_copy(
            send_m.at[slot], recv_m.at[z, core, y_hi, d], m_send, sem,
            device_id={"chan": chan_at(m) - core, "day": day}, device_id_type=MESH,
        ).start()

    for mh in (1, 0):
        for kz in (4, 3, 5, 2, 6, 1, 7, 0):
            if kz or mh:
                mz = lax.rem(z + kz, 8) ^ z
                send_head(0, 2 * mz + mh, m_recv.at[mz])

    recv_t[x] = send_t[x]

    def keep_own(src, k):
        @pl.when(core == 0)
        def _():
            recv_m[z, 0, y_hi, k] = src[...]

        @pl.when(core == 1)
        def _():
            pltpu.make_async_remote_copy(
                src, recv_m.at[z, 1, y_hi, k], s_send, m_recv.at[0],
                device_id={"chan": c - 1}, device_id_type=MESH,
            ).start()

    keep_own(send_m.at[x * 32 + y * 16 + chip], d)

    pl.semaphore_wait(ready, 7)

    order = (4, 5, 7, 6, 3, 2, 1, 0)

    def send_heads(mz):
        def send(r, carry):
            send_head(DAYS - r // 2, 2 * mz + lax.rem(r, 2), m_recv.at[mz])
            return carry

        lax.fori_loop(2, 2 * DAYS, send, 0)

    def join_tails():
        pltpu.make_async_copy(recv_t.at[pl.ds(0, 3)], recv_t.at[pl.ds(0, 3)], t_recv).wait()
        for g in range(4):
            tiles = [recv_t[n, g].astype(F32) for n in range(4)]
            for u in range(4):
                mixed = tiles[u]
                for n in range(4):
                    if n != u:
                        moved = pltpu.roll(tiles[n], (32 * (n - u)) % 128, 1)
                        mixed = jnp.where(group == n, moved, mixed)
                mix_f[pl.ds(4 * g + u, 32, stride=CH), :] = mixed
        send_e[...] = mix_f[...].astype(BF16).reshape(32, 16, 128)
        keep_own(send_e.at[y * 16 + chip], DAYS + y)

    offsets = (4, 3, 5, 2, 6, 1, 7, 0)

    def send_tails(kz):
        mz = lax.rem(z + kz, 8) ^ z

        def send(r, carry):
            h = 1 - r // 2
            m = 2 * mz + 1 - lax.rem(r, 2)
            pltpu.make_async_remote_copy(
                send_e.at[(y ^ h) * 16 + (chip ^ m)], recv_m.at[z, core, y_hi, DAYS + y],
                e_send, m_recv.at[mz],
                device_id={"chan": chan_at(m) - core, "day": d ^ (4 * h)}, device_id_type=MESH,
            ).start()
            return carry

        lax.fori_loop(0, 4 if kz else 3, send, 0)

    def send_day(e):
        for mh in (1, 0):
            for kz in offsets:
                send_head(e, 2 * (lax.rem(z + kz, 8) ^ z) + mh, m_recv.at[lax.rem(z + kz, 8) ^ z])

    for e in (6, 2, 7, 3):
        send_day(e)
    join_tails()
    for e in (5, 1, 4):
        send_day(e)
    for kz in offsets:
        send_tails(kz)

    def far_rows(p):
        for b in range(2):
            for side in range(2):
                for zz in range(2):
                    tiles = recv_m[lax.rem(p, 2) * 4 + 2 * b + zz, side, p // 2]
                    heads = tiles[:DAYS].reshape(DAYS * 16, 128).astype(F32)
                    tails = tiles[DAYS:].reshape(32, 128).astype(F32)
                    heads = (pltpu.roll(heads, 64, 1) * sign64).astype(BF16)
                    tails = (swap16(tails) * sign16).astype(BF16)
                    row = b * 128 + side * 32 + zz * 16
                    far[:, row : row + 16, :] = tiles
                    far[0:DAYS, row + 64 : row + 80, :] = heads.reshape(DAYS, 16, 128)
                    far[DAYS:KB, row + 64 : row + 80, :] = tails.reshape(2, 16, 128)

    def keep(e, m, side):
        day = d ^ e
        pltpu.make_async_remote_copy(
            send_c.at[day, side, chip ^ m], recv_d.at[d, chip], d_send, d_recv.at[e],
            device_id={"chan": chan_at(m) + side, "day": day}, device_id_type=MESH,
        ).start()

    @pl.when(core == 0)
    def _():
        for mz in order:
            some = recv_m.at[z ^ mz] if mz else send_m.at[pl.ds(0, 38)]
            pltpu.make_async_copy(some, some, m_recv.at[mz]).wait()

        for s in (1, 3, 2, 0):
            p = (d // 2) ^ s
            far_rows(p)
            for side in (1, 0):
                near = [recv_m[:, side, :, k].reshape(256, 128) for k in range(KB)]
                prod = lax.dot_general(
                    jnp.concatenate(near, axis=1),
                    jnp.concatenate([far[k] for k in range(KB)], axis=1),
                    NT, preferred_element_type=F32,
                ).astype(BF16)
                for b in range(2):
                    send_c[2 * p + b, side] = prod[:, b * 128 : (b + 1) * 128].reshape(CHIPS, 16, 128)

                for mh in (1, 0):
                    for kz in offsets:
                        mz = lax.rem(z + kz, 8) ^ z

                        def keep_all(r, carry, s=s, side=side, m=2 * mz + mh):
                            keep(2 * s + 1 - r, m, side)
                            return carry

                        if kz or mh:
                            lax.fori_loop(0, 2, keep_all, 0)
                keep(2 * s + 1, 0, side)
                if s or side:
                    keep(2 * s, 0, side)
                else:
                    recv_d[d, chip] = send_c[d, 0, chip]

    def widen(src):
        lag_f[pl.ds(pl.multiple_of(src * 256, 256), 256), :] = (
            recv_d[src].reshape(256, 128).astype(F32)
        )

    for e in (3, 2, 7, 6, 5, 4, 1):
        some = recv_d.at[d ^ e]
        pltpu.make_async_copy(some, some, d_recv.at[e]).wait()
        widen(d ^ e)

    @pl.when(core == 0)
    def _():
        some = recv_d.at[d, pl.ds(0, 15)]
        pltpu.make_async_copy(some, some, d_recv.at[0]).wait()

    @pl.when(core == 1)
    def _():
        some = recv_d.at[d]
        pltpu.make_async_copy(some, some, d_recv.at[0]).wait()

    widen(d)

    tables_copy.wait()
    for n in range(4):
        for u in range(4):
            t = lag_f[pl.ds(n * 4 + u, 128, stride=16), :].astype(BF16).T
            lag_rows[u * 64 : (u + 1) * 64, 0:128] = t[0:64]
            lag_rows[u * 64 : (u + 1) * 64, 128:256] = t[64:128]
        rows = lag_rows[...]
        lags = jnp.dot(rows, tables[0], preferred_element_type=F32)
        lags = lags + jnp.dot(rows, tables[1], preferred_element_type=F32)
        for u in range(4):
            for side in range(2):
                for b in range(2):
                    src = u * 64 + side * 32 + b * 16
                    dst = (b * 32 + side * 16) * 16 + n * 4 + u
                    for h in range(2):
                        out_f[h, pl.ds(dst, 16, stride=16), :] = (
                            lags[src : src + 16, h * 128 : (h + 1) * 128]
                        )
    for h in range(2):
        out_ref[:, h * 128 : (h + 1) * 128] = out_f[h]

    sent = send_t.at[pl.ds(0, 3)]
    pltpu.make_async_copy(sent, sent, t_send).wait()
    sent = send_m.at[pl.ds(0, 127)]
    pltpu.make_async_copy(sent, sent, m_send).wait()
    sent = send_e.at[pl.ds(0, 31)]
    pltpu.make_async_copy(sent, sent, e_send).wait()

    @pl.when(core == 0)
    def _():
        some = send_c.reshape(256, 16, 128).at[pl.ds(0, 255)]
        pltpu.make_async_copy(some, some, d_send).wait()

    @pl.when(core == 1)
    def _():
        some = send_m.at[pl.ds(0, 2)]
        pltpu.make_async_copy(some, some, s_send).wait()


def shards(spectra):
    dma = pltpu.SemaphoreType.DMA
    out = pl.pallas_call(
        kernel,
        out_shape=jax.ShapeDtypeStruct((1024, 256), F32),
        in_specs=[pl.BlockSpec(memory_space=pltpu.HBM)] * 3,
        out_specs=pl.BlockSpec(memory_space=pltpu.VMEM),
        scratch_shapes=[
            pltpu.VMEM((CH, WINDOWS, 2 * BINS), BF16),
            pltpu.VMEM((BINS, 128), F32),
            pltpu.VMEM((2, LAGS, LAGS), BF16),
            pltpu.VMEM((2048, 128), F32),
            pltpu.VMEM((BINS, 16, 128), BF16),
            pltpu.VMEM((4, 4, 32, 128), BF16),
            pltpu.VMEM((4, 4, 32, 128), BF16),
            pltpu.VMEM((512, 128), F32),
            pltpu.VMEM((32, 16, 128), BF16),
            pltpu.VMEM((8, 2, 2, KB, 16, 128), BF16),
            pltpu.VMEM((KB, 256, 128), BF16),
            pltpu.VMEM((DAYS, 2, CHIPS, 16, 128), BF16),
            pltpu.VMEM((DAYS, CHIPS, 16, 128), BF16),
            pltpu.VMEM((2048, 128), F32),
            pltpu.VMEM((256, 256), BF16),
            pltpu.VMEM((2, 1024, 128), F32),
            dma((4,)),
            dma,
            dma,
            pltpu.SemaphoreType.REGULAR,
            dma,
            dma,
            dma,
            dma((8,)),
            dma,
            dma,
            dma,
            dma((DAYS,)),
        ],
        compiler_params=pltpu.CompilerParams(
            collective_id=0, has_side_effects=True, vmem_limit_bytes=40 << 20
        ),
    )(*[
        pltpu.with_memory_space_constraint(v, pltpu.HBM)
        for v in (spectra, jnp.asarray(taper_table()), jnp.asarray(np.stack(lag_tables())))
    ])
    return out.reshape(64, 16, 256)


def solution(mesh):
    return jax.shard_map(
        shards,
        mesh=mesh,
        in_specs=(P("day", "chan", None),),
        out_specs=P("day", "chan"),
        check_vma=False,
    )
```
